32 devices in a mesh: pp: 2 (over y), fsdp: 8 (over z, x), tp: 2 (over core).
Axes of the slice: x: 2, y: 2, z: 4, core: 2. Of those that a mesh axis runs over, the one named last changes fastest.
Arguments:
- saved_inputs: bfloat16 [2, 1024, 8192], P('pp', 'fsdp', 'tp'), may hold values from -6 to 6
- returned: bfloat16 [2, 1024, 8192], P('pp', 'fsdp', 'tp'), may hold values from -6 to 6
- proj_weight: bfloat16 [2, 8192, 640], P('pp', 'tp', 'fsdp'), may hold values from -0.03125 to 0.03125
- log_rate: float32 [2, 128], P('pp', 'tp'), may hold values from -4.6 to -1.2
- step_bias: float32 [2, 128], P('pp', 'tp'), may hold values from -3 to -1
- skip_gain: float32 [2, 128], P('pp', 'tp'), may hold values from 0.5 to 1.5
Outputs:
- grad_out: bfloat16 [2, 1024, 8192], P('pp', 'fsdp', 'tp')
- weight_grad: float32 [2, 8192, 640], P('pp', 'tp', 'fsdp')
The draws below stay inside these ranges and needn't reach their ends.
All inputs are finite; a program needn't handle non-finite values.
Results may differ from the reference program's by a relative error of at most 0.0044.
Values may be sent and summed in bfloat16 or wider, within the bound.
A program may use at most 64 MiB of HBM per device.

```python
import jax
import jax.numpy as jnp
from jax import lax

HEADS = 128
HEAD_DIM = 64
STATE = 256
BLOCK = 128
SEQ_LEN = 128
SECTIONS = 2
TOKENS = 1024
INNER = 8192
PCOLS = 640


def steps_of(key, shape, pieces, least, top_value):
    gain, own = 1.0, jax.random.fold_in(key, 6)
    for dim, parts in pieces:
        steps = jnp.exp(jax.random.uniform(jax.random.fold_in(own, dim), (parts,), jnp.float32, least / len(pieces), top_value / len(pieces)))
        gain = gain * jnp.repeat(steps, shape[dim] // parts).reshape([-1 if axis == dim else 1 for axis in range(len(shape))])
    return gain


def noise(own_key, dims, spread, reach, split=(), held_as=jnp.bfloat16):
    level = steps_of(own_key, dims, split, -0.22, 0.18) if split else 1.0
    result = jax.random.normal(own_key, dims, jnp.float32) * spread * level
    return jnp.minimum(jnp.maximum(result, -reach), reach).astype(held_as)


def setup_inputs(seed: int = 0) -> dict:
    keys = jax.random.split(jax.random.key(seed), 7)
    saved_inputs = noise(keys[0], (SECTIONS, TOKENS, INNER), 1.0, 6.0, ((0, 2), (1, 8), (2, 2)))
    returned = noise(keys[1], (SECTIONS, TOKENS, INNER), 1.0, 6.0, ((0, 2), (1, 8), (2, 2)))
    proj_weight = noise(keys[2], (SECTIONS, INNER, PCOLS), (4 * INNER) ** -0.5, 0.03125, ((0, 2), (1, 2), (2, 8)))
    log_rate = jnp.clip(-4.6 + 3.3999999 * jax.random.uniform(keys[3], (SECTIONS, HEADS), jnp.float32) ** steps_of(keys[3], (SECTIONS, HEADS), ((0, 2), (1, 2)), -0.2, 0.2), -4.6, -1.2)
    step_bias = jnp.clip(-3.0 + 2.0 * jax.random.uniform(keys[4], (SECTIONS, HEADS), jnp.float32) ** steps_of(keys[4], (SECTIONS, HEADS), ((0, 2), (1, 2)), -0.2, 0.2), -3.0, -1.0)
    skip_gain = jnp.clip(0.5 + 1.0 * jax.random.uniform(keys[5], (SECTIONS, HEADS), jnp.float32) ** steps_of(keys[5], (SECTIONS, HEADS), ((0, 2), (1, 2)), -0.2, 0.2), 0.5, 1.5)
    return {"saved_inputs": saved_inputs, "returned": returned, "proj_weight": proj_weight, "log_rate": log_rate, "step_bias": step_bias, "skip_gain": skip_gain}


def state_space(head_input, b_values, c_values, raw_step, log_rate, step_bias, skip_gain):
    length, head_count, head_size = head_input.shape
    blocks = length // BLOCK
    highest = lax.Precision.HIGHEST
    step_size = jax.nn.softplus(raw_step + step_bias[None, :])
    log_decay = -step_size * jnp.exp(log_rate)[None, :]
    block_values = head_input.reshape(blocks, BLOCK, head_count, head_size)
    b_blocks = b_values.reshape(blocks, BLOCK, b_values.shape[1])
    c_blocks = c_values.reshape(blocks, BLOCK, c_values.shape[1])
    cumulative = jnp.cumsum(log_decay.reshape(blocks, BLOCK, head_count), axis=1)
    scaled = block_values * step_size.reshape(blocks, BLOCK, head_count)[..., None]
    scores = jnp.einsum('kin,kjn->kij', c_blocks, b_blocks, precision=highest)
    causal = (jnp.arange(BLOCK)[:, None] >= jnp.arange(BLOCK)[None, :])[None, :, :, None]
    log_gaps = cumulative[:, :, None, :] - cumulative[:, None, :, :]
    mixing = jnp.where(causal, jnp.exp(jnp.where(causal, log_gaps, 0.0)), 0.0) * scores[..., None]
    within = jnp.einsum('kijh,kjhp->kihp', mixing, scaled, precision=highest)
    to_end = jnp.exp(cumulative[:, -1:, :] - cumulative)
    states = jnp.einsum('kjn,kjhp->khnp', b_blocks, scaled * to_end[..., None], precision=highest)
    totals = jnp.exp(cumulative[:, -1, :])

    def advance(running, inputs_pair):
        block_state, block_total = inputs_pair
        return (block_total[:, None, None] * running + block_state, running)
    start_state = jnp.zeros((head_count, b_values.shape[1], head_size), head_input.dtype)
    _, entering = lax.scan(advance, start_state, (states, totals))
    across = jnp.einsum('kin,khnp->kihp', c_blocks, entering, precision=highest) * jnp.exp(cumulative)[..., None]
    output = (within + across).reshape(length, head_count, head_size)
    return output + skip_gain[None, :, None] * head_input

def reference(saved_inputs, returned, proj_weight, log_rate, step_bias, skip_gain):
    incoming = jnp.roll(returned, -1, axis=0)

    def one_section(section_args):
        inputs, cotangent, weight, rates, biases, gains = section_args
        projected = jnp.dot(inputs, weight, preferred_element_type=jnp.float32)
        sequences = inputs.shape[0] // SEQ_LEN
        seq_inputs = inputs.astype(jnp.float32).reshape(sequences, SEQ_LEN, HEADS, HEAD_DIM)
        seq_proj = projected.reshape(sequences, SEQ_LEN, PCOLS)
        seq_cot = cotangent.astype(jnp.float32).reshape(sequences, SEQ_LEN, HEADS, HEAD_DIM)

        def per_sequence(triple):
            values, columns, upstream = triple

            def local_core(head_input, b_values, c_values, raw_step):
                return state_space(head_input, b_values, c_values, raw_step, rates, biases, gains)
            _, backward = jax.vjp(local_core, values, columns[:, :STATE], columns[:, STATE:2 * STATE], columns[:, 2 * STATE:])
            grad_x, grad_b, grad_c, grad_raw = backward(upstream)
            return (grad_x, jnp.concatenate([grad_b, grad_c, grad_raw], axis=1))
        grad_x, proj_grad = lax.map(per_sequence, (seq_inputs, seq_proj, seq_cot))
        proj_grad = proj_grad.reshape(inputs.shape[0], PCOLS).astype(jnp.bfloat16)
        back_proj = jnp.dot(proj_grad, weight.T, preferred_element_type=jnp.float32)
        grad_inputs = (cotangent.astype(jnp.float32) + grad_x.reshape(inputs.shape[0], INNER) + back_proj).astype(jnp.bfloat16)
        section_wgrad = jnp.dot(inputs.T, proj_grad, preferred_element_type=jnp.float32)
        return (grad_inputs, section_wgrad)
    grad_out, weight_grad = lax.map(one_section, (saved_inputs, incoming, proj_weight, log_rate, step_bias, skip_gain))
    return (grad_out, weight_grad)
```

```python
import functools

import jax
import jax.numpy as jnp
from jax import lax
from jax.experimental import pallas as pl
from jax.experimental.pallas import tpu as pltpu
from jax.sharding import PartitionSpec as P

HEAD_DIM = 64
STATE = 256
BLOCK = 128


def shifted(value, axis, by):
    count = lax.axis_size(axis)
    return lax.ppermute(value, axis, [(i, (i + by) % count) for i in range(count)])


def state_space(head_input, b_values, c_values, raw_step, log_rate, step_bias, skip_gain):
    length, head_count, head_size = head_input.shape
    blocks = length // BLOCK
    highest = lax.Precision.HIGHEST
    step_size = jax.nn.softplus(raw_step + step_bias[None, :])
    log_decay = -step_size * jnp.exp(log_rate)[None, :]
    block_values = head_input.reshape(blocks, BLOCK, head_count, head_size)
    b_blocks = b_values.reshape(blocks, BLOCK, b_values.shape[1])
    c_blocks = c_values.reshape(blocks, BLOCK, c_values.shape[1])
    cumulative = jnp.cumsum(log_decay.reshape(blocks, BLOCK, head_count), axis=1)
    scaled = block_values * step_size.reshape(blocks, BLOCK, head_count)[..., None]
    scores = jnp.einsum("kin,kjn->kij", c_blocks, b_blocks, precision=highest)
    causal = (jnp.arange(BLOCK)[:, None] >= jnp.arange(BLOCK)[None, :])[None, :, :, None]
    log_gaps = cumulative[:, :, None, :] - cumulative[:, None, :, :]
    mixing = jnp.where(causal, jnp.exp(jnp.where(causal, log_gaps, 0.0)), 0.0) * scores[..., None]
    within = jnp.einsum("kijh,kjhp->kihp", mixing, scaled, precision=highest)
    to_end = jnp.exp(cumulative[:, -1:, :] - cumulative)
    states = jnp.einsum("kjn,kjhp->khnp", b_blocks, scaled * to_end[..., None], precision=highest)
    totals = jnp.exp(cumulative[:, -1, :])

    def advance(running, inputs_pair):
        block_state, block_total = inputs_pair
        return (block_total[:, None, None] * running + block_state, running)

    start_state = jnp.zeros((head_count, b_values.shape[1], head_size), head_input.dtype)
    _, entering = lax.scan(advance, start_state, (states, totals))
    across = (
        jnp.einsum("kin,khnp->kihp", c_blocks, entering, precision=highest)
        * jnp.exp(cumulative)[..., None]
    )
    output = (within + across).reshape(length, head_count, head_size)
    return output + skip_gain[None, :, None] * head_input


def head_share(partial_sums):
    return lax.psum_scatter(partial_sums, "tp", scatter_dimension=0, tiled=True)


def per_device(saved_inputs, returned, proj_weight, log_rate, step_bias, skip_gain):
    inputs = saved_inputs[0]
    row_count, inner_here = inputs.shape
    heads_here = log_rate.shape[1]
    weight_local = proj_weight[0]
    arrived = shifted(returned, "pp", -1)[0]
    weight_full = lax.all_gather(weight_local, "fsdp", axis=1, tiled=True)
    partial_proj = jnp.dot(inputs, weight_full, preferred_element_type=jnp.float32)
    projected = lax.all_gather(head_share(partial_proj), "tp", axis=0, tiled=True)
    head_total = projected.shape[1] - 2 * STATE
    offset = lax.axis_index("tp") * heads_here
    raw_step = lax.dynamic_slice_in_dim(projected, 2 * STATE + offset, heads_here, 1)
    values = inputs.astype(jnp.float32).reshape(row_count, heads_here, HEAD_DIM)

    def local_core(head_input, b_values, c_values, step_raw):
        return state_space(
            head_input, b_values, c_values, step_raw, log_rate[0], step_bias[0], skip_gain[0]
        )

    _, backward = jax.vjp(
        local_core, values, projected[:, :STATE], projected[:, STATE : 2 * STATE], raw_step
    )
    upstream = arrived.astype(jnp.float32)
    grad_x, grad_b, grad_c, grad_raw = backward(upstream.reshape(row_count, heads_here, HEAD_DIM))
    placed = lax.dynamic_update_slice_in_dim(
        jnp.zeros((row_count, head_total), jnp.float32), grad_raw, offset, 1
    )
    grad_share = head_share(jnp.concatenate([grad_b, grad_c, placed], axis=1)).astype(jnp.bfloat16)
    proj_grad = lax.all_gather(grad_share, "tp", axis=0, tiled=True)
    back_proj = lax.dot_general(
        proj_grad, weight_full, (((1,), (1,)), ((), ())), preferred_element_type=jnp.float32
    )
    grad_inputs = (upstream + grad_x.reshape(row_count, inner_here) + back_proj).astype(
        jnp.bfloat16
    )
    share = lax.psum_scatter(
        lax.dot_general(
            proj_grad, inputs, (((0,), (0,)), ((), ())), preferred_element_type=jnp.float32
        ),
        "fsdp",
        scatter_dimension=0,
        tiled=True,
    )
    section_wgrad = share.T
    return (grad_inputs[None], section_wgrad[None])


MESH = pl.DeviceIdType.MESH
F32 = jnp.float32
BF16 = jnp.bfloat16
GROUP = 8


def fits(mesh):
    return mesh.shape["tp"] == 2 and mesh.shape["fsdp"] == 8


def times(left, right, over, precision=None):
    return lax.dot_general(
        left, right, ((over[:1], over[1:]), ((), ())),
        precision=precision, preferred_element_type=F32,
    )


def fused_kernel(
    line, pairs,
    x_ref, ret_ref, w_ref, rate_ref, bias_ref, gain_ref,
    out_ref, wg_ref,
    arrived, x_other, w_all, proj, proj_tp, proj_theirs, projs,
    dt_s, cum_s, ddt_s, rs_s, ds_s, ds_in, raw_out, raw_in, gx,
    pg_x, pg_in, up_out, dn_out, up_in, dn_in,
    local_sem, ret_sem, x_sem, wz_recv, wz_up, wz_dn, wx_send, wx_recv,
    pj_send, pj_recv, tp_sem, ds_sem, raw_sem, pg_sem, up_send, up_recv, dn_send, dn_recv,
):
    exact = lax.Precision.HIGHEST
    pp_count = lax.axis_size("pp")
    pp, f, tp = lax.axis_index("pp"), lax.axis_index("fsdp"), lax.axis_index("tp")
    z, x = f // 2, f % 2
    width, inner = w_ref.shape
    rows = x_ref.shape[0]
    heads = rate_ref.shape[0]
    last = line - 1
    before = {"pp": lax.rem(pp + pp_count - 1, pp_count)}
    after = {"pp": lax.rem(pp + 1, pp_count)}
    side = {"fsdp": f + 1 - 2 * x}
    core = {"tp": 1 - tp}
    above, below = {"fsdp": f + 2}, {"fsdp": f - 2}

    def remote(src, dst, send, recv, where):
        return pltpu.make_async_remote_copy(
            src_ref=src, dst_ref=dst, send_sem=send, recv_sem=recv,
            device_id=where, device_id_type=MESH,
        )

    barrier = pltpu.get_barrier_semaphore()
    greeted = [side, core, before] + ([after] if pairs > 2 else [])
    for where in greeted:
        pl.semaphore_signal(barrier, inc=1, device_id=where, device_id_type=MESH)

    @pl.when(z > 0)
    def _():
        pl.semaphore_signal(barrier, inc=1, device_id=below, device_id_type=MESH)

    @pl.when(z < last)
    def _():
        pl.semaphore_signal(barrier, inc=1, device_id=above, device_id_type=MESH)

    ends = jnp.where(z > 0, 1, 0) + jnp.where(z < last, 1, 0)
    pl.semaphore_wait(barrier, len(greeted) + ends)

    own_w = pltpu.make_async_copy(w_ref, w_all.at[z, x], local_sem)
    own_w.start()

    def w_up(block, s):
        src = w_ref if s == 0 else w_all.at[block, x]
        return remote(src, w_all.at[block, x], wz_up.at[s], wz_recv.at[block], above)

    def w_dn(block, s):
        src = w_ref if s == 0 else w_all.at[block, x]
        return remote(src, w_all.at[block, x], wz_dn.at[s], wz_recv.at[block], below)

    def w_side(block):
        return remote(
            w_all.at[block, x], w_all.at[block, x], wx_send.at[block], wx_recv.at[block], side
        )

    @pl.when(z < last)
    def _():
        w_up(z, 0).start()

    @pl.when(z > 0)
    def _():
        w_dn(z, 0).start()

    x_copy = remote(x_ref, x_other, x_sem.at[0], x_sem.at[1], side)
    x_copy.start()
    ret_copy = remote(ret_ref, arrived, ret_sem.at[0], ret_sem.at[1], before)
    ret_copy.start()

    def pj_copy(block):
        return remote(
            proj_theirs.at[block], proj.at[block, x], pj_send.at[block], pj_recv.at[block], side
        )

    def project(block):
        weight = w_all[block, x]
        proj_theirs[block] = times(weight, x_other[...], (1, 1))
        pj_copy(block).start()
        proj[block, x] = times(weight, x_ref[...], (1, 1))

    own_w.wait()
    x_copy.wait_recv()
    w_side(z).start()
    project(z)
    for s in range(1, line):
        low, high = z - s, z + s

        @pl.when(low >= 0)
        def _():
            w_dn(low, s - 1).wait_recv()
            if s < line - 1:
                @pl.when(z < last)
                def _():
                    w_up(low, s).start()
            project(low)

        @pl.when(high <= last)
        def _():
            w_up(high, s - 1).wait_recv()
            if s < line - 1:
                @pl.when(z > 0)
                def _():
                    w_dn(high, s).start()
            project(high)

    for block in range(line):
        remote(
            proj_theirs.at[block], proj.at[block, 1 - x], pj_send.at[block], pj_recv.at[block], side
        ).wait_recv()
    tp_copy = remote(proj, proj_tp, tp_sem.at[0], tp_sem.at[1], core)
    tp_copy.start()
    tp_copy.wait_recv()
    projs[...] = (proj[...] + proj_tp[...]).reshape(projs.shape)

    for block in range(line):
        @pl.when(block != z)
        def _():
            w_side(block).start()

    row_at = lax.broadcasted_iota(jnp.int32, (rows, rows), 0)
    column_at = lax.broadcasted_iota(jnp.int32, (rows, rows), 1)
    causal = row_at >= column_at
    lower = causal.astype(F32)
    upper = (row_at <= column_at).astype(F32)
    b_t, c_t = projs[:STATE], projs[STATE : 2 * STATE]
    start = pl.multiple_of(2 * STATE + tp * heads, 8)
    raw = projs[pl.ds(start, heads)] + bias_ref[...]
    step = jnp.maximum(raw, 0.0) + jnp.log1p(jnp.exp(-jnp.abs(raw)))
    decay = -jnp.exp(rate_ref[...])
    groups = heads // GROUP
    cum_s[...] = times(step * decay, upper, (1, 0), exact).reshape(groups, GROUP, rows)
    dt_s[...] = step.reshape(groups, GROUP, rows)
    scores = times(c_t, b_t, (0, 0), exact)
    ds_s[...] = jnp.zeros_like(ds_s)
    pair_lanes = 2 * HEAD_DIM
    lane = lax.broadcasted_iota(jnp.int32, (rows, pair_lanes), 1)
    ret_copy.wait_recv()

    def group_step(g, carry):
        cum_rows = cum_s[g]
        cum_columns = cum_rows.T
        dt_rows = dt_s[g]
        ddt_rows, rs_columns = [], []
        for p in range(GROUP // 2):
            at = pl.multiple_of(g * (GROUP * HEAD_DIM) + p * pair_lanes, pair_lanes)
            g_pair = arrived[:, pl.ds(at, pair_lanes)]
            x_pair = x_ref[:, pl.ds(at, pair_lanes)]
            g_wide = g_pair.astype(F32)
            g_both = jnp.concatenate(
                [
                    jnp.where(lane < HEAD_DIM, g_wide, 0.0).astype(BF16),
                    jnp.where(lane < HEAD_DIM, 0.0, g_wide).astype(BF16),
                ],
                axis=0,
            )
            products = times(g_both, x_pair, (1, 1))
            mixed, ds_part = [], None
            for e in range(2):
                h = 2 * p + e
                dt_row = dt_rows[h : h + 1]
                gap = cum_columns[:, h : h + 1] - cum_rows[h : h + 1]
                mask = jnp.exp(jnp.where(causal, gap, -1e30))
                product = products[e * rows : (e + 1) * rows]
                with_scores = mask * scores
                total = with_scores * product
                ddt_rows.append(jnp.sum(total, axis=0, keepdims=True))
                rs_columns.append(jnp.sum(total * dt_row, axis=1, keepdims=True))
                part = mask * product * dt_row
                ds_part = part if ds_part is None else ds_part + part
                mixed.append((with_scores * dt_row).astype(BF16))
            ds_s[...] += ds_part
            dx = times(jnp.concatenate(mixed, axis=0), g_both, (0, 0))
            gx[:, pl.ds(at, pair_lanes)] = dx + (1.0 + gain_ref[:, pl.ds(at, pair_lanes)]) * g_wide
        ddt_s[g] = jnp.concatenate(ddt_rows, axis=0)
        rs_s[g] = jnp.concatenate(rs_columns, axis=1).T
        return carry

    lax.fori_loop(0, groups, group_step, 0)
    ds_copy = remote(ds_s, ds_in, ds_sem.at[0], ds_sem.at[1], core)
    ds_copy.start()
    ddt = ddt_s[...].reshape(heads, rows)
    d_cum = rs_s[...].reshape(heads, rows) - step * ddt
    d_decay = times(d_cum, lower, (1, 0), exact)
    raw_out[...] = ((ddt + d_decay * decay) * (1.0 / (1.0 + jnp.exp(-raw)))).astype(BF16)
    raw_copy = remote(raw_out, raw_in, raw_sem.at[0], raw_sem.at[1], core)
    raw_copy.start()
    ds_copy.wait_recv()
    ds_total = ds_s[...] + ds_in[...]
    grad_b = times(c_t, ds_total, (1, 0), exact).astype(BF16)
    grad_c = times(b_t, ds_total, (1, 1), exact).astype(BF16)
    raw_copy.wait_recv()
    mine, other = raw_out[...].astype(F32), raw_in[...].astype(F32)
    first = jnp.where(tp == 0, mine, other).astype(BF16)
    second = jnp.where(tp == 0, other, mine).astype(BF16)
    proj_grad = jnp.concatenate([grad_b, grad_c, first, second], axis=0)
    blocks = proj_grad.reshape(line, 2, width, rows)
    pg_x[0] = blocks[:, 0]
    pg_x[1] = blocks[:, 1]
    pg_copy = remote(pg_x.at[1 - x], pg_in, pg_sem.at[0], pg_sem.at[1], side)
    pg_copy.start()
    pg_copy.wait_recv()

    tile = 512

    def partial(block, at):
        return times(pg_x[x, block], x_ref[:, pl.ds(at, tile)], (1, 0)) + times(
            pg_in[block], x_other[:, pl.ds(at, tile)], (1, 0)
        )

    def sums(block, sink, *more):
        def body(i, carry):
            at = pl.multiple_of(i * tile, tile)
            value = partial(block, at)
            for ref in more:
                value = value + ref[block, :, pl.ds(at, tile)].astype(F32)
            sink(at, value)
            return carry

        lax.fori_loop(0, inner // tile, body, 0)

    def up_copy(block):
        return remote(up_out.at[block], up_in.at[block], up_send.at[block], up_recv.at[block], above)

    def dn_copy(block):
        return remote(dn_out.at[block], dn_in.at[block], dn_send.at[block], dn_recv.at[block], below)

    def into(ref, block):
        def sink(at, value):
            ref[block, :, pl.ds(at, tile)] = value.astype(BF16)

        return sink

    @pl.when(z == 0)
    def _():
        for block in range(last, 0, -1):
            sums(block, into(up_out, block))
            up_copy(block).start()

    @pl.when(z == last)
    def _():
        for block in range(last):
            sums(block, into(dn_out, block))
            dn_copy(block).start()

    for block in range(line):
        remote(
            w_all.at[block, x], w_all.at[block, 1 - x], wx_send.at[block], wx_recv.at[block], side
        ).wait_recv()

    turned = proj_grad.astype(F32).T.astype(BF16)

    def back(i, carry):
        at = pl.multiple_of(i * tile, tile)
        weight = w_all[:, :, :, pl.ds(at, tile)].reshape(line * 2 * width, tile)
        out_ref[:, pl.ds(at, tile)] = (
            gx[:, pl.ds(at, tile)] + times(turned, weight, (1, 0))
        ).astype(BF16)
        return carry

    @pl.when(jnp.logical_or(z == 0, z == last))
    def _():
        lax.fori_loop(0, inner // tile, back, 0)

    for k in range(last):
        up_block, dn_block = last - k, k

        @pl.when(jnp.logical_and(z > 0, z < up_block))
        def _():
            dn = remote(
                up_out.at[up_block], up_in.at[up_block], up_send.at[up_block],
                up_recv.at[up_block], below,
            )
            dn.wait_recv()
            sums(up_block, into(up_out, up_block), up_in)
            up_copy(up_block).start()

        @pl.when(jnp.logical_and(z < last, z > dn_block))
        def _():
            up = remote(
                dn_out.at[dn_block], dn_in.at[dn_block], dn_send.at[dn_block],
                dn_recv.at[dn_block], above,
            )
            up.wait_recv()
            sums(dn_block, into(dn_out, dn_block), dn_in)
            dn_copy(dn_block).start()

    @pl.when(jnp.logical_and(z > 0, z < last))
    def _():
        lax.fori_loop(0, inner // tile, back, 0)

    def final(at, value):
        wg_ref[:, pl.ds(at, tile)] = value

    def from_below():
        remote(up_out.at[z], up_in.at[z], up_send.at[z], up_recv.at[z], below).wait_recv()

    def from_above():
        remote(dn_out.at[z], dn_in.at[z], dn_send.at[z], dn_recv.at[z], above).wait_recv()

    @pl.when(z == 0)
    def _():
        from_above()
        sums(z, final, dn_in)

    @pl.when(z == last)
    def _():
        from_below()
        sums(z, final, up_in)

    @pl.when(jnp.logical_and(z > 0, z < last))
    def _():
        from_below()
        from_above()
        sums(z, final, up_in, dn_in)

    for copy in (x_copy, ret_copy, tp_copy, ds_copy, raw_copy, pg_copy):
        copy.wait_send()
    for block in range(line):
        pj_copy(block).wait_send()
        w_side(block).wait_send()

        @pl.when(block > z)
        def _():
            up_copy(block).wait_send()

        @pl.when(block < z)
        def _():
            dn_copy(block).wait_send()

    for s in range(line - 1):
        @pl.when(jnp.logical_and(z < last, z - s >= 0))
        def _():
            w_up(z - s, s).wait_send()

        @pl.when(jnp.logical_and(z > 0, z + s <= last))
        def _():
            w_dn(z + s, s).wait_send()


def fused_device(saved_inputs, returned, proj_weight, log_rate, step_bias, skip_gain):
    inputs = saved_inputs[0]
    rows, inner = inputs.shape
    heads = log_rate.shape[1]
    width = proj_weight.shape[2]
    line = lax.axis_size("fsdp") // 2
    columns = line * 2 * width
    groups = heads // GROUP
    vmem = pl.BlockSpec(memory_space=pltpu.VMEM)
    dma = pltpu.SemaphoreType.DMA
    grad_out, share = pl.pallas_call(
        functools.partial(fused_kernel, line, lax.axis_size("pp")),
        out_shape=(
            jax.ShapeDtypeStruct((rows, inner), BF16),
            jax.ShapeDtypeStruct((width, inner), F32),
        ),
        in_specs=[vmem] * 6,
        out_specs=(vmem, vmem),
        scratch_shapes=[
            pltpu.VMEM((rows, inner), BF16),
            pltpu.VMEM((rows, inner), BF16),
            pltpu.VMEM((line, 2, width, inner), BF16),
            pltpu.VMEM((line, 2, width, rows), F32),
            pltpu.VMEM((line, 2, width, rows), F32),
            pltpu.VMEM((line, width, rows), F32),
            pltpu.VMEM((columns, rows), F32),
            pltpu.VMEM((groups, GROUP, rows), F32),
            pltpu.VMEM((groups, GROUP, rows), F32),
            pltpu.VMEM((groups, GROUP, rows), F32),
            pltpu.VMEM((groups, GROUP, rows), F32),
            pltpu.VMEM((rows, rows), F32),
            pltpu.VMEM((rows, rows), F32),
            pltpu.VMEM((heads, rows), BF16),
            pltpu.VMEM((heads, rows), BF16),
            pltpu.VMEM((rows, inner), F32),
            pltpu.VMEM((2, line, width, rows), BF16),
            pltpu.VMEM((line, width, rows), BF16),
            pltpu.VMEM((line, width, inner), BF16),
            pltpu.VMEM((line, width, inner), BF16),
            pltpu.VMEM((line, width, inner), BF16),
            pltpu.VMEM((line, width, inner), BF16),
            dma, dma((2,)), dma((2,)), dma((line,)), dma((line,)), dma((line,)),
            dma((line,)), dma((line,)), dma((line,)), dma((line,)), dma((2,)), dma((2,)),
            dma((2,)), dma((2,)), dma((line,)), dma((line,)), dma((line,)), dma((line,)),
        ],
        compiler_params=pltpu.CompilerParams(
            collective_id=0, has_side_effects=True, vmem_limit_bytes=48 * 1024 * 1024
        ),
    )(
        inputs,
        returned[0],
        proj_weight[0].T,
        log_rate[0][:, None],
        step_bias[0][:, None],
        jnp.repeat(skip_gain[0], HEAD_DIM)[None, :],
    )
    return (grad_out[None], share.T[None])


def solution(mesh):
    placed = (
        P("pp", "fsdp", "tp"),
        P("pp", "fsdp", "tp"),
        P("pp", "tp", "fsdp"),
        P("pp", "tp"),
        P("pp", "tp"),
        P("pp", "tp"),
    )
    return jax.shard_map(
        fused_device if fits(mesh) else per_device,
        mesh=mesh,
        in_specs=placed,
        out_specs=(P("pp", "fsdp", "tp"), P("pp", "tp", "fsdp")),
        check_vma=False,
    )
```

```python
import functools

import jax
import jax.numpy as jnp
from jax import lax
from jax.experimental import pallas as pl
from jax.experimental.pallas import tpu as pltpu
from jax.sharding import PartitionSpec as P

HEAD_DIM = 64
STATE = 256
BLOCK = 128


def shifted(value, axis, by):
    count = lax.axis_size(axis)
    return lax.ppermute(value, axis, [(i, (i + by) % count) for i in range(count)])


def state_space(head_input, b_values, c_values, raw_step, log_rate, step_bias, skip_gain):
    length, head_count, head_size = head_input.shape
    blocks = length // BLOCK
    highest = lax.Precision.HIGHEST
    step_size = jax.nn.softplus(raw_step + step_bias[None, :])
    log_decay = -step_size * jnp.exp(log_rate)[None, :]
    block_values = head_input.reshape(blocks, BLOCK, head_count, head_size)
    b_blocks = b_values.reshape(blocks, BLOCK, b_values.shape[1])
    c_blocks = c_values.reshape(blocks, BLOCK, c_values.shape[1])
    cumulative = jnp.cumsum(log_decay.reshape(blocks, BLOCK, head_count), axis=1)
    scaled = block_values * step_size.reshape(blocks, BLOCK, head_count)[..., None]
    scores = jnp.einsum("kin,kjn->kij", c_blocks, b_blocks, precision=highest)
    causal = (jnp.arange(BLOCK)[:, None] >= jnp.arange(BLOCK)[None, :])[None, :, :, None]
    log_gaps = cumulative[:, :, None, :] - cumulative[:, None, :, :]
    mixing = jnp.where(causal, jnp.exp(jnp.where(causal, log_gaps, 0.0)), 0.0) * scores[..., None]
    within = jnp.einsum("kijh,kjhp->kihp", mixing, scaled, precision=highest)
    to_end = jnp.exp(cumulative[:, -1:, :] - cumulative)
    states = jnp.einsum("kjn,kjhp->khnp", b_blocks, scaled * to_end[..., None], precision=highest)
    totals = jnp.exp(cumulative[:, -1, :])

    def advance(running, inputs_pair):
        block_state, block_total = inputs_pair
        return (block_total[:, None, None] * running + block_state, running)

    start_state = jnp.zeros((head_count, b_values.shape[1], head_size), head_input.dtype)
    _, entering = lax.scan(advance, start_state, (states, totals))
    across = (
        jnp.einsum("kin,khnp->kihp", c_blocks, entering, precision=highest)
        * jnp.exp(cumulative)[..., None]
    )
    output = (within + across).reshape(length, head_count, head_size)
    return output + skip_gain[None, :, None] * head_input


def head_share(partial_sums):
    return lax.psum_scatter(partial_sums, "tp", scatter_dimension=0, tiled=True)


def per_device(saved_inputs, returned, proj_weight, log_rate, step_bias, skip_gain):
    inputs = saved_inputs[0]
    row_count, inner_here = inputs.shape
    heads_here = log_rate.shape[1]
    weight_local = proj_weight[0]
    arrived = shifted(returned, "pp", -1)[0]
    weight_full = lax.all_gather(weight_local, "fsdp", axis=1, tiled=True)
    partial_proj = jnp.dot(inputs, weight_full, preferred_element_type=jnp.float32)
    projected = lax.all_gather(head_share(partial_proj), "tp", axis=0, tiled=True)
    head_total = projected.shape[1] - 2 * STATE
    offset = lax.axis_index("tp") * heads_here
    raw_step = lax.dynamic_slice_in_dim(projected, 2 * STATE + offset, heads_here, 1)
    values = inputs.astype(jnp.float32).reshape(row_count, heads_here, HEAD_DIM)

    def local_core(head_input, b_values, c_values, step_raw):
        return state_space(
            head_input, b_values, c_values, step_raw, log_rate[0], step_bias[0], skip_gain[0]
        )

    _, backward = jax.vjp(
        local_core, values, projected[:, :STATE], projected[:, STATE : 2 * STATE], raw_step
    )
    upstream = arrived.astype(jnp.float32)
    grad_x, grad_b, grad_c, grad_raw = backward(upstream.reshape(row_count, heads_here, HEAD_DIM))
    placed = lax.dynamic_update_slice_in_dim(
        jnp.zeros((row_count, head_total), jnp.float32), grad_raw, offset, 1
    )
    grad_share = head_share(jnp.concatenate([grad_b, grad_c, placed], axis=1)).astype(jnp.bfloat16)
    proj_grad = lax.all_gather(grad_share, "tp", axis=0, tiled=True)
    back_proj = lax.dot_general(
        proj_grad, weight_full, (((1,), (1,)), ((), ())), preferred_element_type=jnp.float32
    )
    grad_inputs = (upstream + grad_x.reshape(row_count, inner_here) + back_proj).astype(
        jnp.bfloat16
    )
    share = lax.psum_scatter(
        lax.dot_general(
            proj_grad, inputs, (((0,), (0,)), ((), ())), preferred_element_type=jnp.float32
        ),
        "fsdp",
        scatter_dimension=0,
        tiled=True,
    )
    section_wgrad = share.T
    return (grad_inputs[None], section_wgrad[None])


MESH = pl.DeviceIdType.MESH
F32 = jnp.float32
BF16 = jnp.bfloat16
GROUP = 8


def fits(mesh):
    return mesh.shape["tp"] == 2 and mesh.shape["fsdp"] == 8


def times(left, right, over, precision=None):
    return lax.dot_general(
        left, right, ((over[:1], over[1:]), ((), ())),
        precision=precision, preferred_element_type=F32,
    )


def fused_kernel(
    line, pairs,
    x_hbm, ret_ref, w_ref, rate_ref, bias_ref, gain_ref,
    out_ref, wg_ref,
    x_ref, gain_s, xa, pg_z, pg_a, parts, side_out, side_in,
    arrived, x_other, w_all, proj, proj_tp, proj_theirs, projs,
    dt_s, cum_s, ddt_s, rs_s, ds_s, ds_in, raw_out, raw_in, gx,
    pg_x, pg_in, up_out, dn_out, up_in, dn_in,
    local_sem, local_x, local_a, xa_recv, xa_up, xa_dn, pa_send, pa_recv, side_sem, ret_sem, x_sem, wz_recv, wz_up, wz_dn, wx_send, wx_recv,
    pj_send, pj_recv, tp_sem, ds_sem, raw_sem, pg_sem, up_send, up_recv, dn_send, dn_recv,
):
    exact = lax.Precision.HIGHEST
    pp_count = lax.axis_size("pp")
    pp, f, tp = lax.axis_index("pp"), lax.axis_index("fsdp"), lax.axis_index("tp")
    z, x = f // 2, f % 2
    width, inner = w_ref.shape
    rows = x_ref.shape[0]
    heads = rate_ref.shape[1]
    wide = xa.shape[2]
    last = line - 1
    before = {"pp": lax.rem(pp + pp_count - 1, pp_count)}
    after = {"pp": lax.rem(pp + 1, pp_count)}
    side = {"fsdp": f + 1 - 2 * x}
    core = {"tp": 1 - tp}
    above, below = {"fsdp": f + 2}, {"fsdp": f - 2}

    def remote(src, dst, send, recv, where):
        return pltpu.make_async_remote_copy(
            src_ref=src, dst_ref=dst, send_sem=send, recv_sem=recv,
            device_id=where, device_id_type=MESH,
        )

    barrier = pltpu.get_barrier_semaphore()
    greeted = [side, core, before] + ([after] if pairs > 2 else [])
    for where in greeted:
        pl.semaphore_signal(barrier, inc=1, device_id=where, device_id_type=MESH)

    for k in range(1, line):
        along = {"fsdp": 2 * lax.rem(z + k, line) + x}
        pl.semaphore_signal(barrier, inc=1, device_id=along, device_id_type=MESH)
    pl.semaphore_wait(barrier, len(greeted) + line - 1)

    own_w = pltpu.make_async_copy(w_ref, w_all.at[z, x], local_sem)
    own_x = pltpu.make_async_copy(x_hbm, x_ref, local_x)
    own_a = pltpu.make_async_copy(x_hbm.at[:, pl.ds(0, wide)], xa.at[z], local_a)

    def w_up(block, s):
        src = w_ref if s == 0 else w_all.at[block, x]
        return remote(src, w_all.at[block, x], wz_up.at[s], wz_recv.at[block], above)

    def w_dn(block, s):
        src = w_ref if s == 0 else w_all.at[block, x]
        return remote(src, w_all.at[block, x], wz_dn.at[s], wz_recv.at[block], below)

    def w_side(block):
        return remote(
            w_all.at[block, x], w_all.at[block, x], wx_send.at[block], wx_recv.at[block], side
        )

    @pl.when(z < last)
    def _():
        w_up(z, 0).start()

    @pl.when(z > 0)
    def _():
        w_dn(z, 0).start()

    x_copy = remote(x_hbm, x_other, x_sem.at[0], x_sem.at[1], side)
    x_copy.start()
    ret_copy = remote(ret_ref, arrived, ret_sem.at[0], ret_sem.at[1], before)
    ret_copy.start()
    own_w.start()
    own_x.start()
    own_a.start()

    def pj_copy(block):
        return remote(
            proj_theirs.at[block], proj.at[block, x], pj_send.at[block], pj_recv.at[block], side
        )

    def project(block):
        weight = w_all[block, x]
        proj_theirs[block] = times(weight, x_other[...], (1, 1))
        pj_copy(block).start()
        proj[block, x] = times(weight, x_ref[...], (1, 1))

    own_w.wait()
    own_x.wait()
    own_a.wait()
    x_copy.wait_recv()
    w_side(z).start()
    project(z)
    for s in range(1, line):
        low, high = z - s, z + s

        @pl.when(low >= 0)
        def _():
            w_dn(low, s - 1).wait_recv()
            if s < line - 1:
                @pl.when(z < last)
                def _():
                    w_up(low, s).start()
            project(low)

        @pl.when(high <= last)
        def _():
            w_up(high, s - 1).wait_recv()
            if s < line - 1:
                @pl.when(z > 0)
                def _():
                    w_dn(high, s).start()
            project(high)

    def xa_up_copy(block, s):
        return remote(xa.at[block], xa.at[block], xa_up.at[s], xa_recv.at[block], above)

    def xa_dn_copy(block, s):
        return remote(xa.at[block], xa.at[block], xa_dn.at[s], xa_recv.at[block], below)

    def xa_pass(s):
        low, high = z - s, z + s

        @pl.when(low >= 0)
        def _():
            if s > 0:
                xa_dn_copy(low, s - 1).wait_recv()
            if s < line - 1:
                @pl.when(z < last)
                def _():
                    xa_up_copy(low, s).start()

        @pl.when(high <= last)
        def _():
            if s > 0:
                xa_up_copy(high, s - 1).wait_recv()
            if s < line - 1:
                @pl.when(z > 0)
                def _():
                    xa_dn_copy(high, s).start()

    xa_pass(0)
    for block in range(line):
        remote(
            proj_theirs.at[block], proj.at[block, 1 - x], pj_send.at[block], pj_recv.at[block], side
        ).wait_recv()
    tp_copy = remote(proj, proj_tp, tp_sem.at[0], tp_sem.at[1], core)
    tp_copy.start()
    tp_copy.wait_recv()
    projs[...] = (proj[...] + proj_tp[...]).reshape(projs.shape)

    for k in range(1, line - 1):
        w_side(lax.rem(z + k, line)).start()

    row_at = lax.broadcasted_iota(jnp.int32, (rows, rows), 0)
    column_at = lax.broadcasted_iota(jnp.int32, (rows, rows), 1)
    causal = row_at >= column_at
    lower = causal.astype(F32)
    upper = (row_at <= column_at).astype(F32)
    b_t, c_t = projs[:STATE], projs[STATE : 2 * STATE]
    start = pl.multiple_of(2 * STATE + tp * heads, 8)
    raw = projs[pl.ds(start, heads)] + jnp.broadcast_to(bias_ref[...], (rows, heads)).T
    step = jnp.maximum(raw, 0.0) + jnp.log1p(jnp.exp(-jnp.abs(raw)))
    decay = -jnp.exp(jnp.broadcast_to(rate_ref[...], (rows, heads)).T)
    groups = heads // GROUP
    gain_s[...] = jnp.broadcast_to(gain_ref[...], (rows, heads)).T.reshape(groups, GROUP, rows)
    cum_s[...] = times(step * decay, upper, (1, 0), exact).reshape(groups, GROUP, rows)
    dt_s[...] = step.reshape(groups, GROUP, rows)
    scores = times(c_t, b_t, (0, 0), exact)
    ds_s[...] = jnp.zeros_like(ds_s)
    pair_lanes = 2 * HEAD_DIM
    lane = lax.broadcasted_iota(jnp.int32, (rows, pair_lanes), 1)
    ret_copy.wait_recv()

    def group_step(g, carry):
        cum_rows = cum_s[g]
        cum_columns = cum_rows.T
        dt_rows = dt_s[g]
        gain_rows = gain_s[g]

        @pl.when(g == groups // 2)
        def _():
            xa_pass(1)

        ddt_rows, rs_columns = [], []
        for p in range(GROUP // 2):
            at = pl.multiple_of(g * (GROUP * HEAD_DIM) + p * pair_lanes, pair_lanes)
            g_pair = arrived[:, pl.ds(at, pair_lanes)]
            x_pair = x_ref[:, pl.ds(at, pair_lanes)]
            g_wide = g_pair.astype(F32)
            g_both = jnp.concatenate(
                [
                    jnp.where(lane < HEAD_DIM, g_wide, 0.0).astype(BF16),
                    jnp.where(lane < HEAD_DIM, 0.0, g_wide).astype(BF16),
                ],
                axis=0,
            )
            products = times(g_both, x_pair, (1, 1))
            mixed, ds_part = [], None
            for e in range(2):
                h = 2 * p + e
                dt_row = dt_rows[h : h + 1]
                gap = cum_columns[:, h : h + 1] - cum_rows[h : h + 1]
                mask = jnp.exp(jnp.where(causal, gap, -1e30))
                product = products[e * rows : (e + 1) * rows]
                with_scores = mask * scores
                total = with_scores * product
                ddt_rows.append(jnp.sum(total, axis=0, keepdims=True))
                rs_columns.append(jnp.sum(total * dt_row, axis=1, keepdims=True))
                part = mask * product * dt_row
                ds_part = part if ds_part is None else ds_part + part
                mixed.append((with_scores * dt_row).astype(BF16))
            ds_s[...] += ds_part
            dx = times(jnp.concatenate(mixed, axis=0), g_both, (0, 0))
            gain = jnp.where(
                lane[:1] < HEAD_DIM, gain_rows[2 * p : 2 * p + 1], gain_rows[2 * p + 1 : 2 * p + 2]
            )
            gx[:, pl.ds(at, pair_lanes)] = dx + (1.0 + gain) * g_wide
        ddt_s[g] = jnp.concatenate(ddt_rows, axis=0)
        rs_s[g] = jnp.concatenate(rs_columns, axis=1).T
        return carry

    lax.fori_loop(0, groups, group_step, 0)
    ds_copy = remote(ds_s, ds_in, ds_sem.at[0], ds_sem.at[1], core)
    ds_copy.start()
    xa_pass(2)
    ddt = ddt_s[...].reshape(heads, rows)
    d_cum = rs_s[...].reshape(heads, rows) - step * ddt
    d_decay = times(d_cum, lower, (1, 0), exact)
    raw_out[...] = ((ddt + d_decay * decay) * (1.0 / (1.0 + jnp.exp(-raw)))).astype(BF16)
    raw_copy = remote(raw_out, raw_in, raw_sem.at[0], raw_sem.at[1], core)
    raw_copy.start()
    ds_copy.wait_recv()
    ds_total = ds_s[...] + ds_in[...]
    grad_b = times(c_t, ds_total, (1, 0), exact).astype(BF16)
    grad_c = times(b_t, ds_total, (1, 1), exact).astype(BF16)
    raw_copy.wait_recv()
    mine, other = raw_out[...].astype(F32), raw_in[...].astype(F32)
    first = jnp.where(tp == 0, mine, other).astype(BF16)
    second = jnp.where(tp == 0, other, mine).astype(BF16)
    proj_grad = jnp.concatenate([grad_b, grad_c, first, second], axis=0)
    pg_z[...] = proj_grad.reshape(line, 2, width, rows)
    pg_x[...] = jnp.stack([pg_z[:, 0], pg_z[:, 1]], axis=0)
    pg_copy = remote(pg_x.at[1 - x], pg_in, pg_sem.at[0], pg_sem.at[1], side)
    pg_copy.start()

    def pa_copy(k):
        to = lax.rem(z + k, line)
        return remote(
            pg_z.at[to], pg_a.at[z], pa_send.at[k], pa_recv.at[k], {"fsdp": 2 * to + x}
        )

    for k in range(1, line):
        pa_copy(k).start()
    turned = proj_grad.astype(F32).T.astype(BF16)
    pg_a[z] = pg_z[z]
    pg_copy.wait_recv()
    w_side(lax.rem(z + line - 1, line)).start()

    tile = 512
    chunk = parts.shape[3]
    chunks = parts.shape[0]
    both = jnp.concatenate(
        [pg_x[x].reshape(line * width, rows), pg_in[...].reshape(line * width, rows)], axis=1
    )

    def part(c):
        def body(i, carry):
            at = pl.multiple_of(i * tile, tile)
            here = pl.multiple_of(wide + c * chunk + i * tile, tile)
            tokens = jnp.concatenate(
                [x_ref[:, pl.ds(here, tile)], x_other[:, pl.ds(here, tile)]], axis=0
            )
            value = times(both, tokens, (1, 0))
            parts[c, :, :, pl.ds(at, tile)] = value.reshape(line, width, tile)
            return carry

        lax.fori_loop(0, chunk // tile, body, 0)

    def up_copy(c, block, where=above):
        return remote(
            up_out.at[c, block], up_in.at[c, block], up_send.at[c, block], up_recv.at[c, block],
            where,
        )

    def dn_copy(c, block, where=below):
        return remote(
            dn_out.at[c, block], dn_in.at[c, block], dn_send.at[c, block], dn_recv.at[c, block],
            where,
        )

    for c in range(chunks):
        part(c)

        @pl.when(z == 0)
        def _():
            for block in range(last, 0, -1):
                up_out[c, block] = parts[c, block].astype(BF16)
                up_copy(c, block).start()

        @pl.when(z == last)
        def _():
            for block in range(last):
                dn_out[c, block] = parts[c, block].astype(BF16)
                dn_copy(c, block).start()

    for k in range(1, line):
        src = lax.rem(z + line - k, line)
        remote(
            pg_z.at[z], pg_a.at[src], pa_send.at[k], pa_recv.at[k], {"fsdp": 2 * src + x}
        ).wait_recv()
    xa_pass(3)
    mine_a = jnp.concatenate([pg_a[b, x] for b in range(line)], axis=1)
    side_a = jnp.concatenate([pg_a[b, 1 - x] for b in range(line)], axis=1)
    all_a = jnp.concatenate([mine_a, side_a], axis=0)

    def gathered(i, carry):
        at = pl.multiple_of(i * tile, tile)
        tokens = xa[:, :, pl.ds(at, tile)].reshape(line * rows, tile)
        value = times(all_a, tokens, (1, 0))
        wg_ref[:, pl.ds(at, tile)] = value[:width]
        side_out[:, pl.ds(at, tile)] = value[width:].astype(BF16)
        return carry

    lax.fori_loop(0, wide // tile, gathered, 0)
    side_copy = remote(side_out, side_in, side_sem.at[0], side_sem.at[1], side)
    side_copy.start()

    def relay(c):
        for k in range(last):
            up_block, dn_block = last - k, k

            @pl.when(jnp.logical_and(z > 0, z < up_block))
            def _():
                up_copy(c, up_block, below).wait_recv()
                up_out[c, up_block] = (
                    parts[c, up_block] + up_in[c, up_block].astype(F32)
                ).astype(BF16)
                up_copy(c, up_block).start()

            @pl.when(jnp.logical_and(z < last, z > dn_block))
            def _():
                dn_copy(c, dn_block, above).wait_recv()
                dn_out[c, dn_block] = (
                    parts[c, dn_block] + dn_in[c, dn_block].astype(F32)
                ).astype(BF16)
                dn_copy(c, dn_block).start()

    def back(i, carry):
        at = pl.multiple_of(i * tile, tile)
        weight = w_all[:, :, :, pl.ds(at, tile)].reshape(line * 2 * width, tile)
        out_ref[:, pl.ds(at, tile)] = (
            gx[:, pl.ds(at, tile)] + times(turned, weight, (1, 0))
        ).astype(BF16)
        return carry

    for c in range(chunks):
        relay(c)
    for block in range(line):
        remote(
            w_all.at[block, x], w_all.at[block, 1 - x], wx_send.at[block], wx_recv.at[block], side
        ).wait_recv()
    lax.fori_loop(0, inner // tile, back, 0)
    side_copy.wait_recv()
    wg_ref[:, :wide] = wg_ref[:, :wide] + side_in[...].astype(F32)
    for c in range(chunks):
        lanes = slice(wide + c * chunk, wide + (c + 1) * chunk)

        @pl.when(z > 0)
        def _():
            up_copy(c, z, below).wait_recv()

        @pl.when(z < last)
        def _():
            dn_copy(c, z, above).wait_recv()

        @pl.when(z == 0)
        def _():
            wg_ref[:, lanes] = parts[c, z] + dn_in[c, z].astype(F32)

        @pl.when(z == last)
        def _():
            wg_ref[:, lanes] = parts[c, z] + up_in[c, z].astype(F32)

        @pl.when(jnp.logical_and(z > 0, z < last))
        def _():
            wg_ref[:, lanes] = (
                parts[c, z] + up_in[c, z].astype(F32) + dn_in[c, z].astype(F32)
            )

    for copy in (x_copy, ret_copy, tp_copy, ds_copy, raw_copy, pg_copy, side_copy):
        copy.wait_send()
    for block in range(line):
        pj_copy(block).wait_send()
        w_side(block).wait_send()

        for c in range(chunks):
            @pl.when(block > z)
            def _():
                up_copy(c, block).wait_send()

            @pl.when(block < z)
            def _():
                dn_copy(c, block).wait_send()

    for k in range(1, line):
        pa_copy(k).wait_send()

    for s in range(line - 1):
        @pl.when(jnp.logical_and(z < last, z - s >= 0))
        def _():
            w_up(z - s, s).wait_send()
            xa_up_copy(z - s, s).wait_send()

        @pl.when(jnp.logical_and(z > 0, z + s <= last))
        def _():
            w_dn(z + s, s).wait_send()
            xa_dn_copy(z + s, s).wait_send()


def fused_device(saved_inputs, returned, proj_weight, log_rate, step_bias, skip_gain):
    inputs = saved_inputs[0]
    rows, inner = inputs.shape
    heads = log_rate.shape[1]
    width = proj_weight.shape[2]
    line = lax.axis_size("fsdp") // 2
    columns = line * 2 * width
    groups = heads // GROUP
    wide = inner // 2
    chunks, chunk = 2, (inner - wide) // 2
    vmem = pl.BlockSpec(memory_space=pltpu.VMEM)
    dma = pltpu.SemaphoreType.DMA
    grad_out, share = pl.pallas_call(
        functools.partial(fused_kernel, line, lax.axis_size("pp")),
        out_shape=(
            jax.ShapeDtypeStruct((rows, inner), BF16),
            jax.ShapeDtypeStruct((width, inner), F32),
        ),
        in_specs=[pl.BlockSpec(memory_space=pl.ANY)] * 3 + [vmem] * 3,
        out_specs=(vmem, vmem),
        scratch_shapes=[
            pltpu.VMEM((rows, inner), BF16),
            pltpu.VMEM((groups, GROUP, rows), F32),
            pltpu.VMEM((line, rows, wide), BF16),
            pltpu.VMEM((line, 2, width, rows), BF16),
            pltpu.VMEM((line, 2, width, rows), BF16),
            pltpu.VMEM((chunks, line, width, chunk), F32),
            pltpu.VMEM((width, wide), BF16),
            pltpu.VMEM((width, wide), BF16),
            pltpu.VMEM((rows, inner), BF16),
            pltpu.VMEM((rows, inner), BF16),
            pltpu.VMEM((line, 2, width, inner), BF16),
            pltpu.VMEM((line, 2, width, rows), F32),
            pltpu.VMEM((line, 2, width, rows), F32),
            pltpu.VMEM((line, width, rows), F32),
            pltpu.VMEM((columns, rows), F32),
            pltpu.VMEM((groups, GROUP, rows), F32),
            pltpu.VMEM((groups, GROUP, rows), F32),
            pltpu.VMEM((groups, GROUP, rows), F32),
            pltpu.VMEM((groups, GROUP, rows), F32),
            pltpu.VMEM((rows, rows), F32),
            pltpu.VMEM((rows, rows), F32),
            pltpu.VMEM((heads, rows), BF16),
            pltpu.VMEM((heads, rows), BF16),
            pltpu.VMEM((rows, inner), F32),
            pltpu.VMEM((2, line, width, rows), BF16),
            pltpu.VMEM((line, width, rows), BF16),
            pltpu.VMEM((chunks, line, width, chunk), BF16),
            pltpu.VMEM((chunks, line, width, chunk), BF16),
            pltpu.VMEM((chunks, line, width, chunk), BF16),
            pltpu.VMEM((chunks, line, width, chunk), BF16),
            dma, dma, dma, dma((line,)), dma((line,)), dma((line,)), dma((line,)), dma((line,)), dma((2,)),
            dma((2,)), dma((2,)), dma((line,)), dma((line,)), dma((line,)),
            dma((line,)), dma((line,)), dma((line,)), dma((line,)), dma((2,)), dma((2,)),
            dma((2,)), dma((2,)), dma((chunks, line)), dma((chunks, line)), dma((chunks, line)),
            dma((chunks, line)),
        ],
        compiler_params=pltpu.CompilerParams(
            collective_id=0, has_side_effects=True, vmem_limit_bytes=60 * 1024 * 1024
        ),
    )(
        inputs,
        returned[0],
        proj_weight[0].T,
        log_rate,
        step_bias,
        skip_gain,
    )
    return (grad_out[None], share.T[None])


def solution(mesh):
    placed = (
        P("pp", "fsdp", "tp"),
        P("pp", "fsdp", "tp"),
        P("pp", "tp", "fsdp"),
        P("pp", "tp"),
        P("pp", "tp"),
        P("pp", "tp"),
    )
    return jax.shard_map(
        fused_device if fits(mesh) else per_device,
        mesh=mesh,
        in_specs=placed,
        out_specs=(P("pp", "fsdp", "tp"), P("pp", "tp", "fsdp")),
        check_vma=False,
    )
```

```python
import functools

import jax
import jax.numpy as jnp
from jax import lax
from jax.experimental import pallas as pl
from jax.experimental.pallas import tpu as pltpu
from jax.sharding import PartitionSpec as P

HEAD_DIM = 64
STATE = 256
BLOCK = 128


def shifted(value, axis, by):
    count = lax.axis_size(axis)
    return lax.ppermute(value, axis, [(i, (i + by) % count) for i in range(count)])


def state_space(head_input, b_values, c_values, raw_step, log_rate, step_bias, skip_gain):
    length, head_count, head_size = head_input.shape
    blocks = length // BLOCK
    highest = lax.Precision.HIGHEST
    step_size = jax.nn.softplus(raw_step + step_bias[None, :])
    log_decay = -step_size * jnp.exp(log_rate)[None, :]
    block_values = head_input.reshape(blocks, BLOCK, head_count, head_size)
    b_blocks = b_values.reshape(blocks, BLOCK, b_values.shape[1])
    c_blocks = c_values.reshape(blocks, BLOCK, c_values.shape[1])
    cumulative = jnp.cumsum(log_decay.reshape(blocks, BLOCK, head_count), axis=1)
    scaled = block_values * step_size.reshape(blocks, BLOCK, head_count)[..., None]
    scores = jnp.einsum("kin,kjn->kij", c_blocks, b_blocks, precision=highest)
    causal = (jnp.arange(BLOCK)[:, None] >= jnp.arange(BLOCK)[None, :])[None, :, :, None]
    log_gaps = cumulative[:, :, None, :] - cumulative[:, None, :, :]
    mixing = jnp.where(causal, jnp.exp(jnp.where(causal, log_gaps, 0.0)), 0.0) * scores[..., None]
    within = jnp.einsum("kijh,kjhp->kihp", mixing, scaled, precision=highest)
    to_end = jnp.exp(cumulative[:, -1:, :] - cumulative)
    states = jnp.einsum("kjn,kjhp->khnp", b_blocks, scaled * to_end[..., None], precision=highest)
    totals = jnp.exp(cumulative[:, -1, :])

    def advance(running, inputs_pair):
        block_state, block_total = inputs_pair
        return (block_total[:, None, None] * running + block_state, running)

    start_state = jnp.zeros((head_count, b_values.shape[1], head_size), head_input.dtype)
    _, entering = lax.scan(advance, start_state, (states, totals))
    across = (
        jnp.einsum("kin,khnp->kihp", c_blocks, entering, precision=highest)
        * jnp.exp(cumulative)[..., None]
    )
    output = (within + across).reshape(length, head_count, head_size)
    return output + skip_gain[None, :, None] * head_input


def head_share(partial_sums):
    return lax.psum_scatter(partial_sums, "tp", scatter_dimension=0, tiled=True)


def per_device(saved_inputs, returned, proj_weight, log_rate, step_bias, skip_gain):
    inputs = saved_inputs[0]
    row_count, inner_here = inputs.shape
    heads_here = log_rate.shape[1]
    weight_local = proj_weight[0]
    arrived = shifted(returned, "pp", -1)[0]
    weight_full = lax.all_gather(weight_local, "fsdp", axis=1, tiled=True)
    partial_proj = jnp.dot(inputs, weight_full, preferred_element_type=jnp.float32)
    projected = lax.all_gather(head_share(partial_proj), "tp", axis=0, tiled=True)
    head_total = projected.shape[1] - 2 * STATE
    offset = lax.axis_index("tp") * heads_here
    raw_step = lax.dynamic_slice_in_dim(projected, 2 * STATE + offset, heads_here, 1)
    values = inputs.astype(jnp.float32).reshape(row_count, heads_here, HEAD_DIM)

    def local_core(head_input, b_values, c_values, step_raw):
        return state_space(
            head_input, b_values, c_values, step_raw, log_rate[0], step_bias[0], skip_gain[0]
        )

    _, backward = jax.vjp(
        local_core, values, projected[:, :STATE], projected[:, STATE : 2 * STATE], raw_step
    )
    upstream = arrived.astype(jnp.float32)
    grad_x, grad_b, grad_c, grad_raw = backward(upstream.reshape(row_count, heads_here, HEAD_DIM))
    placed = lax.dynamic_update_slice_in_dim(
        jnp.zeros((row_count, head_total), jnp.float32), grad_raw, offset, 1
    )
    grad_share = head_share(jnp.concatenate([grad_b, grad_c, placed], axis=1)).astype(jnp.bfloat16)
    proj_grad = lax.all_gather(grad_share, "tp", axis=0, tiled=True)
    back_proj = lax.dot_general(
        proj_grad, weight_full, (((1,), (1,)), ((), ())), preferred_element_type=jnp.float32
    )
    grad_inputs = (upstream + grad_x.reshape(row_count, inner_here) + back_proj).astype(
        jnp.bfloat16
    )
    share = lax.psum_scatter(
        lax.dot_general(
            proj_grad, inputs, (((0,), (0,)), ((), ())), preferred_element_type=jnp.float32
        ),
        "fsdp",
        scatter_dimension=0,
        tiled=True,
    )
    section_wgrad = share.T
    return (grad_inputs[None], section_wgrad[None])


MESH = pl.DeviceIdType.MESH
F32 = jnp.float32
BF16 = jnp.bfloat16
GROUP = 8


def fits(mesh):
    return mesh.shape["tp"] == 2 and mesh.shape["fsdp"] == 8


def times(left, right, over, precision=None):
    return lax.dot_general(
        left, right, ((over[:1], over[1:]), ((), ())),
        precision=precision, preferred_element_type=F32,
    )


def fused_kernel(
    line, pairs,
    x_hbm, ret_ref, w_ref, rate_ref, bias_ref, gain_ref,
    out_ref, wg_ref,
    x_ref, gain_s, xa, pg_z, pg_a, parts, side_out, side_in,
    arrived, x_other, w_all, proj, proj_tp, proj_theirs, projs,
    shift_s, cum_s, dshift_s, rs_s, ds_s, ds_in, raw_out, raw_in, gx,
    pg_x, pg_in, up_out, dn_out, up_in, dn_in,
    local_sem, local_x, local_a, xa_recv, xa_up, xa_dn, pa_send, pa_recv, side_sem, ret_sem, x_sem, wz_recv, wz_up, wz_dn, wx_send, wx_recv,
    pj_send, pj_recv, tp_sem, ds_sem, raw_sem, pg_sem, up_send, up_recv, dn_send, dn_recv,
):
    exact = lax.Precision.HIGHEST
    pp_count = lax.axis_size("pp")
    pp, f, tp = lax.axis_index("pp"), lax.axis_index("fsdp"), lax.axis_index("tp")
    z, x = f // 2, f % 2
    width, inner = w_ref.shape
    rows = x_ref.shape[0]
    heads = rate_ref.shape[1]
    wide = xa.shape[2]
    last = line - 1
    before = {"pp": lax.rem(pp + pp_count - 1, pp_count)}
    after = {"pp": lax.rem(pp + 1, pp_count)}
    side = {"fsdp": f + 1 - 2 * x}
    core = {"tp": 1 - tp}
    above, below = {"fsdp": f + 2}, {"fsdp": f - 2}

    def remote(src, dst, send, recv, where):
        return pltpu.make_async_remote_copy(
            src_ref=src, dst_ref=dst, send_sem=send, recv_sem=recv,
            device_id=where, device_id_type=MESH,
        )

    barrier = pltpu.get_barrier_semaphore()
    greeted = [side, core, before] + ([after] if pairs > 2 else [])
    for where in greeted:
        pl.semaphore_signal(barrier, inc=1, device_id=where, device_id_type=MESH)

    for k in range(1, line):
        along = {"fsdp": 2 * lax.rem(z + k, line) + x}
        pl.semaphore_signal(barrier, inc=1, device_id=along, device_id_type=MESH)
    pl.semaphore_wait(barrier, len(greeted) + line - 1)

    own_w = pltpu.make_async_copy(w_ref, w_all.at[z, x], local_sem)
    own_x = pltpu.make_async_copy(x_hbm, x_ref, local_x)
    own_a = pltpu.make_async_copy(x_hbm.at[:, pl.ds(0, wide)], xa.at[z], local_a)

    def w_up(block, s):
        src = w_ref if s == 0 else w_all.at[block, x]
        return remote(src, w_all.at[block, x], wz_up.at[s], wz_recv.at[block], above)

    def w_dn(block, s):
        src = w_ref if s == 0 else w_all.at[block, x]
        return remote(src, w_all.at[block, x], wz_dn.at[s], wz_recv.at[block], below)

    def w_side(block):
        return remote(
            w_all.at[block, x], w_all.at[block, x], wx_send.at[block], wx_recv.at[block], side
        )

    @pl.when(z < last)
    def _():
        w_up(z, 0).start()

    @pl.when(z > 0)
    def _():
        w_dn(z, 0).start()

    x_copy = remote(x_hbm, x_other, x_sem.at[0], x_sem.at[1], side)
    x_copy.start()
    ret_copy = remote(ret_ref, arrived, ret_sem.at[0], ret_sem.at[1], before)
    ret_copy.start()
    own_w.start()
    own_x.start()
    own_a.start()

    def pj_copy(block):
        return remote(
            proj_theirs.at[block], proj.at[block, x], pj_send.at[block], pj_recv.at[block], side
        )

    def project(block):
        weight = w_all[block, x]
        proj_theirs[block] = times(weight, x_other[...], (1, 1))
        pj_copy(block).start()
        proj[block, x] = times(weight, x_ref[...], (1, 1))

    def xa_up_copy(block, s):
        return remote(xa.at[block], xa.at[block], xa_up.at[s], xa_recv.at[block], above)

    def xa_dn_copy(block, s):
        return remote(xa.at[block], xa.at[block], xa_dn.at[s], xa_recv.at[block], below)

    def xa_pass(s):
        low, high = z - s, z + s

        @pl.when(low >= 0)
        def _():
            xa_dn_copy(low, s - 1).wait_recv()
            if s < line - 1:
                @pl.when(z < last)
                def _():
                    xa_up_copy(low, s).start()

        @pl.when(high <= last)
        def _():
            xa_up_copy(high, s - 1).wait_recv()
            if s < line - 1:
                @pl.when(z > 0)
                def _():
                    xa_dn_copy(high, s).start()

    def w_pass(s):
        low, high = z - s, z + s

        @pl.when(low >= 0)
        def _():
            w_dn(low, s - 1).wait_recv()
            if s < line - 1:
                @pl.when(z < last)
                def _():
                    w_up(low, s).start()

        @pl.when(high <= last)
        def _():
            w_up(high, s - 1).wait_recv()
            if s < line - 1:
                @pl.when(z > 0)
                def _():
                    w_dn(high, s).start()

        @pl.when(jnp.logical_and(z == s - 1, z < last))
        def _():
            xa_up_copy(z, 0).start()

        @pl.when(jnp.logical_and(z == last + 1 - s, z > 0))
        def _():
            xa_dn_copy(z, 0).start()

    def project_at(s):
        @pl.when(z - s >= 0)
        def _():
            project(z - s)

        @pl.when(z + s <= last)
        def _():
            project(z + s)

    own_w.wait()
    own_x.wait()
    own_a.wait()
    w_pass(1)
    x_copy.wait_recv()
    w_side(z).start()
    project(z)
    w_pass(2)
    project_at(1)
    for s in range(3, line):
        w_pass(s)
        project_at(s - 1)
    project_at(line - 1)
    for block in range(line):
        remote(
            proj_theirs.at[block], proj.at[block, 1 - x], pj_send.at[block], pj_recv.at[block], side
        ).wait_recv()
    tp_copy = remote(proj, proj_tp, tp_sem.at[0], tp_sem.at[1], core)
    tp_copy.start()
    tp_copy.wait_recv()
    projs[...] = (proj[...] + proj_tp[...]).reshape(projs.shape)

    for k in range(1, line - 1):
        w_side(lax.rem(z + k, line)).start()

    row_at = lax.broadcasted_iota(jnp.int32, (rows, rows), 0)
    column_at = lax.broadcasted_iota(jnp.int32, (rows, rows), 1)
    lower = (row_at >= column_at).astype(F32)
    causal = row_at <= column_at
    upper = (row_at <= column_at).astype(F32)
    b_t, c_t = projs[:STATE], projs[STATE : 2 * STATE]
    start = pl.multiple_of(2 * STATE + tp * heads, 8)
    raw = projs[pl.ds(start, heads)] + jnp.broadcast_to(bias_ref[...], (rows, heads)).T
    step = jnp.maximum(raw, 0.0) + jnp.log1p(jnp.exp(-jnp.abs(raw)))
    decay = -jnp.exp(jnp.broadcast_to(rate_ref[...], (rows, heads)).T)
    groups = heads // GROUP
    gain_s[...] = jnp.broadcast_to(gain_ref[...], (rows, heads)).T.reshape(groups, GROUP, rows)
    cumulative = times(step * decay, upper, (1, 0), exact)
    cum_s[...] = cumulative.reshape(groups, GROUP, rows)
    shift_s[...] = (cumulative - jnp.log(step)).reshape(groups, GROUP, rows)
    head_of = lax.broadcasted_iota(jnp.int32, (GROUP, GROUP * HEAD_DIM), 1) // HEAD_DIM
    picks = (head_of == lax.broadcasted_iota(jnp.int32, head_of.shape, 0)).astype(F32).astype(BF16)
    scores = times(b_t, c_t, (0, 0), exact)
    scores = jnp.concatenate([scores, scores], axis=1)
    ds_s[...] = jnp.zeros_like(ds_s)
    pair_lanes = 2 * HEAD_DIM
    lane = lax.broadcasted_iota(jnp.int32, (rows, pair_lanes), 1)
    ret_copy.wait_recv()

    def group_step(g, carry):
        cum_rows = cum_s[g]
        shift_columns = shift_s[g].T
        gain_rows = gain_s[g]

        @pl.when(g == groups // 4)
        def _():
            xa_pass(1)

        rs_rows, shares, ds_part = [], [], None
        for p in range(GROUP // 2):
            at = pl.multiple_of(g * (GROUP * HEAD_DIM) + p * pair_lanes, pair_lanes)
            g_wide = arrived[:, pl.ds(at, pair_lanes)].astype(F32)
            x_pair = x_ref[:, pl.ds(at, pair_lanes)]
            g_both = jnp.concatenate(
                [
                    jnp.where(lane < HEAD_DIM, g_wide, 0.0).astype(BF16),
                    jnp.where(lane < HEAD_DIM, 0.0, g_wide).astype(BF16),
                ],
                axis=0,
            )
            products = times(x_pair, g_both, (1, 1))
            masks = []
            for h in (2 * p, 2 * p + 1):
                gap = cum_rows[h : h + 1] - shift_columns[:, h : h + 1]
                masks.append(jnp.exp(jnp.where(causal, gap, -1e30)))
            mask = jnp.concatenate(masks, axis=1)
            mixed = mask * scores
            sums = jnp.sum(mixed * products, axis=0, keepdims=True)
            rs_rows += [sums[:, :rows], sums[:, rows:]]
            weighted = mask * products
            weighted = weighted[:, :rows] + weighted[:, rows:]
            ds_part = weighted if ds_part is None else ds_part + weighted
            dx = times(mixed.astype(BF16), g_both, (1, 0))
            gain = jnp.where(
                lane[:1] < HEAD_DIM, gain_rows[2 * p : 2 * p + 1], gain_rows[2 * p + 1 : 2 * p + 2]
            )
            gx[:, pl.ds(at, pair_lanes)] = dx + (1.0 + gain) * g_wide
            shares.append(dx * x_pair.astype(F32))
        ds_s[...] += ds_part
        share = jnp.concatenate(shares, axis=1)
        high = share.astype(BF16)
        low = (share - high.astype(F32)).astype(BF16)
        dshift_s[g] = times(picks, high, (1, 1)) + times(picks, low, (1, 1))
        rs_s[g] = jnp.concatenate(rs_rows, axis=0)
        return carry

    lax.fori_loop(0, groups, group_step, 0)
    ds_copy = remote(ds_s, ds_in, ds_sem.at[0], ds_sem.at[1], core)
    ds_copy.start()
    xa_pass(2)
    ddt = dshift_s[...].reshape(heads, rows)
    d_cum = rs_s[...].reshape(heads, rows) - ddt
    d_decay = times(d_cum, lower, (1, 0), exact)
    slope = jnp.exp(jnp.minimum(raw, 0.0)) / (1.0 + jnp.exp(-jnp.abs(raw)))
    ratio = jnp.where(step > 1e-30, slope / jnp.maximum(step, 1e-30), 1.0)
    raw_out[...] = (ddt * ratio + d_decay * decay * slope).astype(BF16)
    raw_copy = remote(raw_out, raw_in, raw_sem.at[0], raw_sem.at[1], core)
    raw_copy.start()
    ds_copy.wait_recv()
    ds_total = ds_s[...] + ds_in[...]
    grad_b = times(c_t, ds_total, (1, 1), exact).astype(BF16)
    grad_c = times(b_t, ds_total, (1, 0), exact).astype(BF16)
    raw_copy.wait_recv()
    mine, other = raw_out[...].astype(F32), raw_in[...].astype(F32)
    first = jnp.where(tp == 0, mine, other).astype(BF16)
    second = jnp.where(tp == 0, other, mine).astype(BF16)
    proj_grad = jnp.concatenate([grad_b, grad_c, first, second], axis=0)
    pg_z[...] = proj_grad.reshape(line, 2, width, rows)
    pg_x[...] = jnp.stack([pg_z[:, 0], pg_z[:, 1]], axis=0)
    pg_copy = remote(pg_x.at[1 - x], pg_in, pg_sem.at[0], pg_sem.at[1], side)
    pg_copy.start()

    def pa_copy(k):
        to = lax.rem(z + k, line)
        return remote(
            pg_z.at[to], pg_a.at[z], pa_send.at[k], pa_recv.at[k], {"fsdp": 2 * to + x}
        )

    for k in range(1, line):
        pa_copy(k).start()
    turned = proj_grad.astype(F32).T.astype(BF16)
    pg_a[z] = pg_z[z]
    pg_copy.wait_recv()
    w_side(lax.rem(z + line - 1, line)).start()

    tile = 512
    chunk = parts.shape[3]
    chunks = parts.shape[0]
    both = jnp.concatenate(
        [pg_x[x].reshape(line * width, rows), pg_in[...].reshape(line * width, rows)], axis=1
    )

    def part(c):
        def body(i, carry):
            at = pl.multiple_of(i * tile, tile)
            here = pl.multiple_of(wide + c * chunk + i * tile, tile)
            tokens = jnp.concatenate(
                [x_ref[:, pl.ds(here, tile)], x_other[:, pl.ds(here, tile)]], axis=0
            )
            value = times(both, tokens, (1, 0))
            parts[c, :, :, pl.ds(at, tile)] = value.reshape(line, width, tile)
            return carry

        lax.fori_loop(0, chunk // tile, body, 0)

    def up_copy(c, block, where=above):
        return remote(
            up_out.at[c, block], up_in.at[c, block], up_send.at[c, block], up_recv.at[c, block],
            where,
        )

    def dn_copy(c, block, where=below):
        return remote(
            dn_out.at[c, block], dn_in.at[c, block], dn_send.at[c, block], dn_recv.at[c, block],
            where,
        )

    for c in range(chunks):
        part(c)

        @pl.when(z == 0)
        def _():
            for block in range(last, 0, -1):
                up_out[c, block] = parts[c, block].astype(BF16)
                up_copy(c, block).start()

        @pl.when(z == last)
        def _():
            for block in range(last):
                dn_out[c, block] = parts[c, block].astype(BF16)
                dn_copy(c, block).start()

    for k in range(1, line):
        src = lax.rem(z + line - k, line)
        remote(
            pg_z.at[z], pg_a.at[src], pa_send.at[k], pa_recv.at[k], {"fsdp": 2 * src + x}
        ).wait_recv()
    xa_pass(3)
    mine_a = jnp.concatenate([pg_a[b, x] for b in range(line)], axis=1)
    side_a = jnp.concatenate([pg_a[b, 1 - x] for b in range(line)], axis=1)
    all_a = jnp.concatenate([mine_a, side_a], axis=0)

    def gathered(i, carry):
        at = pl.multiple_of(i * tile, tile)
        tokens = xa[:, :, pl.ds(at, tile)].reshape(line * rows, tile)
        value = times(all_a, tokens, (1, 0))
        wg_ref[:, pl.ds(at, tile)] = value[:width]
        side_out[:, pl.ds(at, tile)] = value[width:].astype(BF16)
        return carry

    lax.fori_loop(0, wide // tile, gathered, 0)
    side_copy = remote(side_out, side_in, side_sem.at[0], side_sem.at[1], side)
    side_copy.start()

    def relay(c):
        for k in range(last):
            up_block, dn_block = last - k, k

            @pl.when(jnp.logical_and(z > 0, z < up_block))
            def _():
                up_copy(c, up_block, below).wait_recv()
                up_out[c, up_block] = (
                    parts[c, up_block] + up_in[c, up_block].astype(F32)
                ).astype(BF16)
                up_copy(c, up_block).start()

            @pl.when(jnp.logical_and(z < last, z > dn_block))
            def _():
                dn_copy(c, dn_block, above).wait_recv()
                dn_out[c, dn_block] = (
                    parts[c, dn_block] + dn_in[c, dn_block].astype(F32)
                ).astype(BF16)
                dn_copy(c, dn_block).start()

    def back(i, carry):
        at = pl.multiple_of(i * tile, tile)
        weight = w_all[:, :, :, pl.ds(at, tile)].reshape(line * 2 * width, tile)
        out_ref[:, pl.ds(at, tile)] = (
            gx[:, pl.ds(at, tile)] + times(turned, weight, (1, 0))
        ).astype(BF16)
        return carry

    for c in range(chunks):
        relay(c)
    for block in range(line):
        remote(
            w_all.at[block, x], w_all.at[block, 1 - x], wx_send.at[block], wx_recv.at[block], side
        ).wait_recv()
    lax.fori_loop(0, inner // tile, back, 0)
    side_copy.wait_recv()
    wg_ref[:, :wide] = wg_ref[:, :wide] + side_in[...].astype(F32)
    for c in range(chunks):
        lanes = slice(wide + c * chunk, wide + (c + 1) * chunk)

        @pl.when(z > 0)
        def _():
            up_copy(c, z, below).wait_recv()

        @pl.when(z < last)
        def _():
            dn_copy(c, z, above).wait_recv()

        @pl.when(z == 0)
        def _():
            wg_ref[:, lanes] = parts[c, z] + dn_in[c, z].astype(F32)

        @pl.when(z == last)
        def _():
            wg_ref[:, lanes] = parts[c, z] + up_in[c, z].astype(F32)

        @pl.when(jnp.logical_and(z > 0, z < last))
        def _():
            wg_ref[:, lanes] = (
                parts[c, z] + up_in[c, z].astype(F32) + dn_in[c, z].astype(F32)
            )

    for copy in (x_copy, ret_copy, tp_copy, ds_copy, raw_copy, pg_copy, side_copy):
        copy.wait_send()
    for block in range(line):
        pj_copy(block).wait_send()
        w_side(block).wait_send()

        for c in range(chunks):
            @pl.when(block > z)
            def _():
                up_copy(c, block).wait_send()

            @pl.when(block < z)
            def _():
                dn_copy(c, block).wait_send()

    for k in range(1, line):
        pa_copy(k).wait_send()

    for s in range(line - 1):
        @pl.when(jnp.logical_and(z < last, z - s >= 0))
        def _():
            w_up(z - s, s).wait_send()
            xa_up_copy(z - s, s).wait_send()

        @pl.when(jnp.logical_and(z > 0, z + s <= last))
        def _():
            w_dn(z + s, s).wait_send()
            xa_dn_copy(z + s, s).wait_send()


def fused_device(saved_inputs, returned, proj_weight, log_rate, step_bias, skip_gain):
    inputs = saved_inputs[0]
    rows, inner = inputs.shape
    heads = log_rate.shape[1]
    width = proj_weight.shape[2]
    line = lax.axis_size("fsdp") // 2
    columns = line * 2 * width
    groups = heads // GROUP
    wide = inner // 2
    chunks, chunk = 2, (inner - wide) // 2
    vmem = pl.BlockSpec(memory_space=pltpu.VMEM)
    dma = pltpu.SemaphoreType.DMA
    grad_out, share = pl.pallas_call(
        functools.partial(fused_kernel, line, lax.axis_size("pp")),
        out_shape=(
            jax.ShapeDtypeStruct((rows, inner), BF16),
            jax.ShapeDtypeStruct((width, inner), F32),
        ),
        in_specs=[pl.BlockSpec(memory_space=pl.ANY)] * 3 + [vmem] * 3,
        out_specs=(vmem, vmem),
        scratch_shapes=[
            pltpu.VMEM((rows, inner), BF16),
            pltpu.VMEM((groups, GROUP, rows), F32),
            pltpu.VMEM((line, rows, wide), BF16),
            pltpu.VMEM((line, 2, width, rows), BF16),
            pltpu.VMEM((line, 2, width, rows), BF16),
            pltpu.VMEM((chunks, line, width, chunk), F32),
            pltpu.VMEM((width, wide), BF16),
            pltpu.VMEM((width, wide), BF16),
            pltpu.VMEM((rows, inner), BF16),
            pltpu.VMEM((rows, inner), BF16),
            pltpu.VMEM((line, 2, width, inner), BF16),
            pltpu.VMEM((line, 2, width, rows), F32),
            pltpu.VMEM((line, 2, width, rows), F32),
            pltpu.VMEM((line, width, rows), F32),
            pltpu.VMEM((columns, rows), F32),
            pltpu.VMEM((groups, GROUP, rows), F32),
            pltpu.VMEM((groups, GROUP, rows), F32),
            pltpu.VMEM((groups, GROUP, rows), F32),
            pltpu.VMEM((groups, GROUP, rows), F32),
            pltpu.VMEM((rows, rows), F32),
            pltpu.VMEM((rows, rows), F32),
            pltpu.VMEM((heads, rows), BF16),
            pltpu.VMEM((heads, rows), BF16),
            pltpu.VMEM((rows, inner), F32),
            pltpu.VMEM((2, line, width, rows), BF16),
            pltpu.VMEM((line, width, rows), BF16),
            pltpu.VMEM((chunks, line, width, chunk), BF16),
            pltpu.VMEM((chunks, line, width, chunk), BF16),
            pltpu.VMEM((chunks, line, width, chunk), BF16),
            pltpu.VMEM((chunks, line, width, chunk), BF16),
            dma, dma, dma, dma((line,)), dma((line,)), dma((line,)), dma((line,)), dma((line,)), dma((2,)),
            dma((2,)), dma((2,)), dma((line,)), dma((line,)), dma((line,)),
            dma((line,)), dma((line,)), dma((line,)), dma((line,)), dma((2,)), dma((2,)),
            dma((2,)), dma((2,)), dma((chunks, line)), dma((chunks, line)), dma((chunks, line)),
            dma((chunks, line)),
        ],
        compiler_params=pltpu.CompilerParams(
            collective_id=0, has_side_effects=True, vmem_limit_bytes=60 * 1024 * 1024
        ),
    )(
        inputs,
        returned[0],
        proj_weight[0].T,
        log_rate,
        step_bias,
        skip_gain,
    )
    return (grad_out[None], share.T[None])


def solution(mesh):
    placed = (
        P("pp", "fsdp", "tp"),
        P("pp", "fsdp", "tp"),
        P("pp", "tp", "fsdp"),
        P("pp", "tp"),
        P("pp", "tp"),
        P("pp", "tp"),
    )
    return jax.shard_map(
        fused_device if fits(mesh) else per_device,
        mesh=mesh,
        in_specs=placed,
        out_specs=(P("pp", "fsdp", "tp"), P("pp", "tp", "fsdp")),
        check_vma=False,
    )
```

```python
import functools

import jax
import jax.numpy as jnp
from jax import lax
from jax.experimental import pallas as pl
from jax.experimental.pallas import tpu as pltpu
from jax.sharding import PartitionSpec as P

HEAD_DIM = 64
STATE = 256
BLOCK = 128


def shifted(value, axis, by):
    count = lax.axis_size(axis)
    return lax.ppermute(value, axis, [(i, (i + by) % count) for i in range(count)])


def state_space(head_input, b_values, c_values, raw_step, log_rate, step_bias, skip_gain):
    length, head_count, head_size = head_input.shape
    blocks = length // BLOCK
    highest = lax.Precision.HIGHEST
    step_size = jax.nn.softplus(raw_step + step_bias[None, :])
    log_decay = -step_size * jnp.exp(log_rate)[None, :]
    block_values = head_input.reshape(blocks, BLOCK, head_count, head_size)
    b_blocks = b_values.reshape(blocks, BLOCK, b_values.shape[1])
    c_blocks = c_values.reshape(blocks, BLOCK, c_values.shape[1])
    cumulative = jnp.cumsum(log_decay.reshape(blocks, BLOCK, head_count), axis=1)
    scaled = block_values * step_size.reshape(blocks, BLOCK, head_count)[..., None]
    scores = jnp.einsum("kin,kjn->kij", c_blocks, b_blocks, precision=highest)
    causal = (jnp.arange(BLOCK)[:, None] >= jnp.arange(BLOCK)[None, :])[None, :, :, None]
    log_gaps = cumulative[:, :, None, :] - cumulative[:, None, :, :]
    mixing = jnp.where(causal, jnp.exp(jnp.where(causal, log_gaps, 0.0)), 0.0) * scores[..., None]
    within = jnp.einsum("kijh,kjhp->kihp", mixing, scaled, precision=highest)
    to_end = jnp.exp(cumulative[:, -1:, :] - cumulative)
    states = jnp.einsum("kjn,kjhp->khnp", b_blocks, scaled * to_end[..., None], precision=highest)
    totals = jnp.exp(cumulative[:, -1, :])

    def advance(running, inputs_pair):
        block_state, block_total = inputs_pair
        return (block_total[:, None, None] * running + block_state, running)

    start_state = jnp.zeros((head_count, b_values.shape[1], head_size), head_input.dtype)
    _, entering = lax.scan(advance, start_state, (states, totals))
    across = (
        jnp.einsum("kin,khnp->kihp", c_blocks, entering, precision=highest)
        * jnp.exp(cumulative)[..., None]
    )
    output = (within + across).reshape(length, head_count, head_size)
    return output + skip_gain[None, :, None] * head_input


def head_share(partial_sums):
    return lax.psum_scatter(partial_sums, "tp", scatter_dimension=0, tiled=True)


def per_device(saved_inputs, returned, proj_weight, log_rate, step_bias, skip_gain):
    inputs = saved_inputs[0]
    row_count, inner_here = inputs.shape
    heads_here = log_rate.shape[1]
    weight_local = proj_weight[0]
    arrived = shifted(returned, "pp", -1)[0]
    weight_full = lax.all_gather(weight_local, "fsdp", axis=1, tiled=True)
    partial_proj = jnp.dot(inputs, weight_full, preferred_element_type=jnp.float32)
    projected = lax.all_gather(head_share(partial_proj), "tp", axis=0, tiled=True)
    head_total = projected.shape[1] - 2 * STATE
    offset = lax.axis_index("tp") * heads_here
    raw_step = lax.dynamic_slice_in_dim(projected, 2 * STATE + offset, heads_here, 1)
    values = inputs.astype(jnp.float32).reshape(row_count, heads_here, HEAD_DIM)

    def local_core(head_input, b_values, c_values, step_raw):
        return state_space(
            head_input, b_values, c_values, step_raw, log_rate[0], step_bias[0], skip_gain[0]
        )

    _, backward = jax.vjp(
        local_core, values, projected[:, :STATE], projected[:, STATE : 2 * STATE], raw_step
    )
    upstream = arrived.astype(jnp.float32)
    grad_x, grad_b, grad_c, grad_raw = backward(upstream.reshape(row_count, heads_here, HEAD_DIM))
    placed = lax.dynamic_update_slice_in_dim(
        jnp.zeros((row_count, head_total), jnp.float32), grad_raw, offset, 1
    )
    grad_share = head_share(jnp.concatenate([grad_b, grad_c, placed], axis=1)).astype(jnp.bfloat16)
    proj_grad = lax.all_gather(grad_share, "tp", axis=0, tiled=True)
    back_proj = lax.dot_general(
        proj_grad, weight_full, (((1,), (1,)), ((), ())), preferred_element_type=jnp.float32
    )
    grad_inputs = (upstream + grad_x.reshape(row_count, inner_here) + back_proj).astype(
        jnp.bfloat16
    )
    share = lax.psum_scatter(
        lax.dot_general(
            proj_grad, inputs, (((0,), (0,)), ((), ())), preferred_element_type=jnp.float32
        ),
        "fsdp",
        scatter_dimension=0,
        tiled=True,
    )
    section_wgrad = share.T
    return (grad_inputs[None], section_wgrad[None])


MESH = pl.DeviceIdType.MESH
F32 = jnp.float32
BF16 = jnp.bfloat16
GROUP = 8


def fits(mesh):
    return mesh.shape["tp"] == 2 and mesh.shape["fsdp"] == 8


def times(left, right, over, precision=None):
    return lax.dot_general(
        left, right, ((over[:1], over[1:]), ((), ())),
        precision=precision, preferred_element_type=F32,
    )


def fused_kernel(
    line, pairs,
    x_hbm, ret_ref, w_ref, rate_ref, bias_ref, gain_ref,
    out_ref, wg_ref,
    x_ref, gain_s, xa, pg_z, pg_a, parts, side_out, side_in, bp_out, bp_in,
    arrived, x_other, w_all, proj, proj_tp, proj_theirs, projs,
    shift_s, cum_s, dshift_s, rs_s, ds_s, ds_in, raw_out, raw_in, gx,
    pg_x, pg_in, up_out, dn_out, up_in, dn_in,
    local_sem, local_x, local_a, xa_recv, xa_up, xa_dn, pa_send, pa_recv, side_sem, bp_sem, ret_sem, x_sem, wz_recv, wz_up, wz_dn, wx_send, wx_recv,
    pj_send, pj_recv, tp_sem, ds_sem, raw_sem, pg_sem, up_send, up_recv, dn_send, dn_recv,
):
    exact = lax.Precision.HIGHEST
    pp_count = lax.axis_size("pp")
    pp, f, tp = lax.axis_index("pp"), lax.axis_index("fsdp"), lax.axis_index("tp")
    z, x = f // 2, f % 2
    width, inner = w_ref.shape
    rows = x_ref.shape[0]
    heads = rate_ref.shape[1]
    wide = xa.shape[2]
    last = line - 1
    before = {"pp": lax.rem(pp + pp_count - 1, pp_count)}
    after = {"pp": lax.rem(pp + 1, pp_count)}
    side = {"fsdp": f + 1 - 2 * x}
    core = {"tp": 1 - tp}
    above, below = {"fsdp": f + 2}, {"fsdp": f - 2}

    def remote(src, dst, send, recv, where):
        return pltpu.make_async_remote_copy(
            src_ref=src, dst_ref=dst, send_sem=send, recv_sem=recv,
            device_id=where, device_id_type=MESH,
        )

    barrier = pltpu.get_barrier_semaphore()
    greeted = [side, core, before] + ([after] if pairs > 2 else [])
    for where in greeted:
        pl.semaphore_signal(barrier, inc=1, device_id=where, device_id_type=MESH)

    for k in range(1, line):
        along = {"fsdp": 2 * lax.rem(z + k, line) + x}
        pl.semaphore_signal(barrier, inc=1, device_id=along, device_id_type=MESH)
    pl.semaphore_wait(barrier, len(greeted) + line - 1)

    own_w = pltpu.make_async_copy(w_ref, w_all.at[z, x], local_sem)
    own_x = pltpu.make_async_copy(x_hbm, x_ref, local_x)
    own_a = pltpu.make_async_copy(x_hbm.at[:, pl.ds(0, wide)], xa.at[z], local_a)

    def w_up(block, s):
        src = w_ref if s == 0 else w_all.at[block, x]
        return remote(src, w_all.at[block, x], wz_up.at[s], wz_recv.at[block], above)

    def w_dn(block, s):
        src = w_ref if s == 0 else w_all.at[block, x]
        return remote(src, w_all.at[block, x], wz_dn.at[s], wz_recv.at[block], below)

    def w_side(block, column=x):
        half = w_all.at[block, column, :, pl.ds(0, wide)]
        return remote(half, half, wx_send.at[block], wx_recv.at[block], side)

    @pl.when(z < last)
    def _():
        w_up(z, 0).start()

    @pl.when(z > 0)
    def _():
        w_dn(z, 0).start()

    x_copy = remote(x_hbm, x_other, x_sem.at[0], x_sem.at[1], side)
    x_copy.start()
    ret_copy = remote(ret_ref, arrived, ret_sem.at[0], ret_sem.at[1], before)
    ret_copy.start()
    own_w.start()
    own_x.start()
    own_a.start()

    def pj_copy(block):
        return remote(
            proj_theirs.at[block], proj.at[block, x], pj_send.at[block], pj_recv.at[block], side
        )

    def project(block):
        weight = w_all[block, x]
        proj_theirs[block] = times(weight, x_other[...], (1, 1))
        pj_copy(block).start()
        proj[block, x] = times(weight, x_ref[...], (1, 1))

    def xa_up_copy(block, s):
        return remote(xa.at[block], xa.at[block], xa_up.at[s], xa_recv.at[block], above)

    def xa_dn_copy(block, s):
        return remote(xa.at[block], xa.at[block], xa_dn.at[s], xa_recv.at[block], below)

    def xa_pass(s):
        low, high = z - s, z + s

        @pl.when(low >= 0)
        def _():
            xa_dn_copy(low, s - 1).wait_recv()
            if s < line - 1:
                @pl.when(z < last)
                def _():
                    xa_up_copy(low, s).start()

        @pl.when(high <= last)
        def _():
            xa_up_copy(high, s - 1).wait_recv()
            if s < line - 1:
                @pl.when(z > 0)
                def _():
                    xa_dn_copy(high, s).start()

    def w_pass(s):
        low, high = z - s, z + s

        @pl.when(low >= 0)
        def _():
            w_dn(low, s - 1).wait_recv()
            if s < line - 1:
                @pl.when(z < last)
                def _():
                    w_up(low, s).start()

        @pl.when(high <= last)
        def _():
            w_up(high, s - 1).wait_recv()
            if s < line - 1:
                @pl.when(z > 0)
                def _():
                    w_dn(high, s).start()

        @pl.when(jnp.logical_and(z == s - 1, z < last))
        def _():
            xa_up_copy(z, 0).start()

        @pl.when(jnp.logical_and(z == last + 1 - s, z > 0))
        def _():
            xa_dn_copy(z, 0).start()

    def project_at(s):
        @pl.when(z - s >= 0)
        def _():
            project(z - s)

        @pl.when(z + s <= last)
        def _():
            project(z + s)

    own_w.wait()
    own_x.wait()
    own_a.wait()
    w_pass(1)
    x_copy.wait_recv()
    w_side(z).start()
    project(z)
    for low_or_high in (z - 1, z + 1):
        @pl.when(jnp.logical_and(low_or_high >= 0, low_or_high <= last))
        def _():
            w_side(low_or_high).start()

    w_pass(2)
    project_at(1)
    for s in range(3, line):
        w_pass(s)
        project_at(s - 1)
    project_at(line - 1)
    for block in range(line):
        remote(
            proj_theirs.at[block], proj.at[block, 1 - x], pj_send.at[block], pj_recv.at[block], side
        ).wait_recv()
    tp_copy = remote(proj, proj_tp, tp_sem.at[0], tp_sem.at[1], core)
    tp_copy.start()
    tp_copy.wait_recv()
    projs[...] = (proj[...] + proj_tp[...]).reshape(projs.shape)

    for block in range(line):
        @pl.when(jnp.logical_or(block > z + 1, block < z - 1))
        def _():
            w_side(block).start()

    row_at = lax.broadcasted_iota(jnp.int32, (rows, rows), 0)
    column_at = lax.broadcasted_iota(jnp.int32, (rows, rows), 1)
    lower = (row_at >= column_at).astype(F32)
    causal = row_at <= column_at
    upper = (row_at <= column_at).astype(F32)
    b_t, c_t = projs[:STATE], projs[STATE : 2 * STATE]
    start = pl.multiple_of(2 * STATE + tp * heads, 8)
    raw = projs[pl.ds(start, heads)] + jnp.broadcast_to(bias_ref[...], (rows, heads)).T
    step = jnp.maximum(raw, 0.0) + jnp.log1p(jnp.exp(-jnp.abs(raw)))
    decay = -jnp.exp(jnp.broadcast_to(rate_ref[...], (rows, heads)).T)
    groups = heads // GROUP
    gain_s[...] = jnp.broadcast_to(gain_ref[...], (rows, heads)).T.reshape(groups, GROUP, rows)
    cumulative = times(step * decay, upper, (1, 0), exact)
    cum_s[...] = cumulative.reshape(groups, GROUP, rows)
    shift_s[...] = (cumulative - jnp.log(step)).reshape(groups, GROUP, rows)
    head_of = lax.broadcasted_iota(jnp.int32, (GROUP, GROUP * HEAD_DIM), 1) // HEAD_DIM
    picks = (head_of == lax.broadcasted_iota(jnp.int32, head_of.shape, 0)).astype(F32).astype(BF16)
    scores = times(b_t, c_t, (0, 0), exact)
    scores = jnp.concatenate([scores, scores], axis=1)
    ds_s[...] = jnp.zeros_like(ds_s)
    pair_lanes = 2 * HEAD_DIM
    lane = lax.broadcasted_iota(jnp.int32, (rows, pair_lanes), 1)
    ret_copy.wait_recv()

    def group_step(g, carry):
        cum_rows = cum_s[g]
        shift_columns = shift_s[g].T
        gain_rows = gain_s[g]

        @pl.when(g == groups // 4)
        def _():
            xa_pass(1)

        rs_rows, shares, ds_part = [], [], None
        for p in range(GROUP // 2):
            at = pl.multiple_of(g * (GROUP * HEAD_DIM) + p * pair_lanes, pair_lanes)
            g_wide = arrived[:, pl.ds(at, pair_lanes)].astype(F32)
            x_pair = x_ref[:, pl.ds(at, pair_lanes)]
            g_both = jnp.concatenate(
                [
                    jnp.where(lane < HEAD_DIM, g_wide, 0.0).astype(BF16),
                    jnp.where(lane < HEAD_DIM, 0.0, g_wide).astype(BF16),
                ],
                axis=0,
            )
            products = times(x_pair, g_both, (1, 1))
            masks = []
            for h in (2 * p, 2 * p + 1):
                gap = cum_rows[h : h + 1] - shift_columns[:, h : h + 1]
                masks.append(jnp.exp(jnp.where(causal, gap, -1e30)))
            mask = jnp.concatenate(masks, axis=1)
            mixed = mask * scores
            sums = jnp.sum(mixed * products, axis=0, keepdims=True)
            rs_rows += [sums[:, :rows], sums[:, rows:]]
            weighted = mask * products
            weighted = weighted[:, :rows] + weighted[:, rows:]
            ds_part = weighted if ds_part is None else ds_part + weighted
            dx = times(mixed.astype(BF16), g_both, (1, 0))
            gain = jnp.where(
                lane[:1] < HEAD_DIM, gain_rows[2 * p : 2 * p + 1], gain_rows[2 * p + 1 : 2 * p + 2]
            )
            gx[:, pl.ds(at, pair_lanes)] = dx + (1.0 + gain) * g_wide
            shares.append(dx * x_pair.astype(F32))
        ds_s[...] += ds_part
        share = jnp.concatenate(shares, axis=1)
        high = share.astype(BF16)
        low = (share - high.astype(F32)).astype(BF16)
        dshift_s[g] = times(picks, high, (1, 1)) + times(picks, low, (1, 1))
        rs_s[g] = jnp.concatenate(rs_rows, axis=0)
        return carry

    lax.fori_loop(0, groups, group_step, 0)
    ds_copy = remote(ds_s, ds_in, ds_sem.at[0], ds_sem.at[1], core)
    ds_copy.start()
    xa_pass(2)
    ddt = dshift_s[...].reshape(heads, rows)
    d_cum = rs_s[...].reshape(heads, rows) - ddt
    d_decay = times(d_cum, lower, (1, 0), exact)
    slope = jnp.exp(jnp.minimum(raw, 0.0)) / (1.0 + jnp.exp(-jnp.abs(raw)))
    ratio = jnp.where(step > 1e-30, slope / jnp.maximum(step, 1e-30), 1.0)
    raw_out[...] = (ddt * ratio + d_decay * decay * slope).astype(BF16)
    raw_copy = remote(raw_out, raw_in, raw_sem.at[0], raw_sem.at[1], core)
    raw_copy.start()
    ds_copy.wait_recv()
    ds_total = ds_s[...] + ds_in[...]
    grad_b = times(c_t, ds_total, (1, 1), exact).astype(BF16)
    grad_c = times(b_t, ds_total, (1, 0), exact).astype(BF16)
    raw_copy.wait_recv()
    mine, other = raw_out[...].astype(F32), raw_in[...].astype(F32)
    first = jnp.where(tp == 0, mine, other).astype(BF16)
    second = jnp.where(tp == 0, other, mine).astype(BF16)
    proj_grad = jnp.concatenate([grad_b, grad_c, first, second], axis=0)
    pg_z[...] = proj_grad.reshape(line, 2, width, rows)
    pg_x[...] = jnp.stack([pg_z[:, 0], pg_z[:, 1]], axis=0)
    pg_copy = remote(pg_x.at[1 - x], pg_in, pg_sem.at[0], pg_sem.at[1], side)
    pg_copy.start()

    def pa_copy(k):
        to = lax.rem(z + k, line)
        return remote(
            pg_z.at[to], pg_a.at[z], pa_send.at[k], pa_recv.at[k], {"fsdp": 2 * to + x}
        )

    for k in range(1, line):
        pa_copy(k).start()
    turned = proj_grad.astype(F32).T.astype(BF16)
    pg_a[z] = pg_z[z]
    pg_copy.wait_recv()

    tile = 512
    chunk = parts.shape[3]
    chunks = parts.shape[0]
    both = jnp.concatenate(
        [pg_x[x].reshape(line * width, rows), pg_in[...].reshape(line * width, rows)], axis=1
    )

    def part(c):
        def body(i, carry):
            at = pl.multiple_of(i * tile, tile)
            here = pl.multiple_of(wide + c * chunk + i * tile, tile)
            tokens = jnp.concatenate(
                [x_ref[:, pl.ds(here, tile)], x_other[:, pl.ds(here, tile)]], axis=0
            )
            value = times(both, tokens, (1, 0))
            parts[c, :, :, pl.ds(at, tile)] = value.reshape(line, width, tile)
            return carry

        lax.fori_loop(0, chunk // tile, body, 0)

    def turn(value):
        return value.reshape(line * width, rows).astype(F32).T.astype(BF16)

    bp_copy = remote(bp_out, bp_in, bp_sem.at[0], bp_sem.at[1], side)
    turned_in = turn(pg_in[...])
    turned_own = turn(pg_x[x])

    def back_other(i, carry):
        at = pl.multiple_of(i * tile, tile)
        far = pl.multiple_of(wide + i * tile, tile)
        weight = w_all[:, x, :, pl.ds(far, tile)].reshape(line * width, tile)
        bp_out[:, pl.ds(at, tile)] = times(turned_in, weight, (1, 0)).astype(BF16)
        return carry

    def up_copy(c, block, where=above):
        return remote(
            up_out.at[c, block], up_in.at[c, block], up_send.at[c, block], up_recv.at[c, block],
            where,
        )

    def dn_copy(c, block, where=below):
        return remote(
            dn_out.at[c, block], dn_in.at[c, block], dn_send.at[c, block], dn_recv.at[c, block],
            where,
        )

    for c in range(chunks):
        part(c)

        @pl.when(z == 0)
        def _():
            for block in range(last, 0, -1):
                up_out[c, block] = parts[c, block].astype(BF16)
                up_copy(c, block).start()

        @pl.when(z == last)
        def _():
            for block in range(last):
                dn_out[c, block] = parts[c, block].astype(BF16)
                dn_copy(c, block).start()

    lax.fori_loop(0, (inner - wide) // tile, back_other, 0)
    bp_copy.start()
    for k in range(1, line):
        src = lax.rem(z + line - k, line)
        remote(
            pg_z.at[z], pg_a.at[src], pa_send.at[k], pa_recv.at[k], {"fsdp": 2 * src + x}
        ).wait_recv()
    xa_pass(3)
    mine_a = jnp.concatenate([pg_a[b, x] for b in range(line)], axis=1)
    side_a = jnp.concatenate([pg_a[b, 1 - x] for b in range(line)], axis=1)
    all_a = jnp.concatenate([mine_a, side_a], axis=0)

    def gathered(i, carry):
        at = pl.multiple_of(i * tile, tile)
        tokens = xa[:, :, pl.ds(at, tile)].reshape(line * rows, tile)
        value = times(all_a, tokens, (1, 0))
        wg_ref[:, pl.ds(at, tile)] = value[:width]
        side_out[:, pl.ds(at, tile)] = value[width:].astype(BF16)
        return carry

    lax.fori_loop(0, wide // tile, gathered, 0)
    side_copy = remote(side_out, side_in, side_sem.at[0], side_sem.at[1], side)
    side_copy.start()

    def relay(c):
        for k in range(last):
            up_block, dn_block = last - k, k

            @pl.when(jnp.logical_and(z > 0, z < up_block))
            def _():
                up_copy(c, up_block, below).wait_recv()
                up_out[c, up_block] = (
                    parts[c, up_block] + up_in[c, up_block].astype(F32)
                ).astype(BF16)
                up_copy(c, up_block).start()

            @pl.when(jnp.logical_and(z < last, z > dn_block))
            def _():
                dn_copy(c, dn_block, above).wait_recv()
                dn_out[c, dn_block] = (
                    parts[c, dn_block] + dn_in[c, dn_block].astype(F32)
                ).astype(BF16)
                dn_copy(c, dn_block).start()

    def back(i, carry):
        at = pl.multiple_of(i * tile, tile)
        weight = w_all[:, :, :, pl.ds(at, tile)].reshape(line * 2 * width, tile)
        out_ref[:, pl.ds(at, tile)] = (
            gx[:, pl.ds(at, tile)] + times(turned, weight, (1, 0))
        ).astype(BF16)
        return carry

    for c in range(chunks):
        relay(c)
    for block in range(line):
        w_side(block, 1 - x).wait_recv()
    lax.fori_loop(0, wide // tile, back, 0)
    bp_copy.wait_recv()

    def back_far(i, carry):
        at = pl.multiple_of(i * tile, tile)
        far = pl.multiple_of(wide + i * tile, tile)
        weight = w_all[:, x, :, pl.ds(far, tile)].reshape(line * width, tile)
        out_ref[:, pl.ds(far, tile)] = (
            gx[:, pl.ds(far, tile)]
            + times(turned_own, weight, (1, 0))
            + bp_in[:, pl.ds(at, tile)].astype(F32)
        ).astype(BF16)
        return carry

    lax.fori_loop(0, (inner - wide) // tile, back_far, 0)
    side_copy.wait_recv()
    wg_ref[:, :wide] = wg_ref[:, :wide] + side_in[...].astype(F32)
    for c in range(chunks):
        lanes = slice(wide + c * chunk, wide + (c + 1) * chunk)

        @pl.when(z > 0)
        def _():
            up_copy(c, z, below).wait_recv()

        @pl.when(z < last)
        def _():
            dn_copy(c, z, above).wait_recv()

        @pl.when(z == 0)
        def _():
            wg_ref[:, lanes] = parts[c, z] + dn_in[c, z].astype(F32)

        @pl.when(z == last)
        def _():
            wg_ref[:, lanes] = parts[c, z] + up_in[c, z].astype(F32)

        @pl.when(jnp.logical_and(z > 0, z < last))
        def _():
            wg_ref[:, lanes] = (
                parts[c, z] + up_in[c, z].astype(F32) + dn_in[c, z].astype(F32)
            )

    for copy in (x_copy, ret_copy, tp_copy, ds_copy, raw_copy, pg_copy, side_copy, bp_copy):
        copy.wait_send()
    for block in range(line):
        pj_copy(block).wait_send()
        w_side(block).wait_send()

        for c in range(chunks):
            @pl.when(block > z)
            def _():
                up_copy(c, block).wait_send()

            @pl.when(block < z)
            def _():
                dn_copy(c, block).wait_send()

    for k in range(1, line):
        pa_copy(k).wait_send()

    for s in range(line - 1):
        @pl.when(jnp.logical_and(z < last, z - s >= 0))
        def _():
            w_up(z - s, s).wait_send()
            xa_up_copy(z - s, s).wait_send()

        @pl.when(jnp.logical_and(z > 0, z + s <= last))
        def _():
            w_dn(z + s, s).wait_send()
            xa_dn_copy(z + s, s).wait_send()


def fused_device(saved_inputs, returned, proj_weight, log_rate, step_bias, skip_gain):
    inputs = saved_inputs[0]
    rows, inner = inputs.shape
    heads = log_rate.shape[1]
    width = proj_weight.shape[2]
    line = lax.axis_size("fsdp") // 2
    columns = line * 2 * width
    groups = heads // GROUP
    wide = inner // 2
    chunks, chunk = 2, (inner - wide) // 2
    vmem = pl.BlockSpec(memory_space=pltpu.VMEM)
    dma = pltpu.SemaphoreType.DMA
    grad_out, share = pl.pallas_call(
        functools.partial(fused_kernel, line, lax.axis_size("pp")),
        out_shape=(
            jax.ShapeDtypeStruct((rows, inner), BF16),
            jax.ShapeDtypeStruct((width, inner), F32),
        ),
        in_specs=[pl.BlockSpec(memory_space=pl.ANY)] * 3 + [vmem] * 3,
        out_specs=(vmem, vmem),
        scratch_shapes=[
            pltpu.VMEM((rows, inner), BF16),
            pltpu.VMEM((groups, GROUP, rows), F32),
            pltpu.VMEM((line, rows, wide), BF16),
            pltpu.VMEM((line, 2, width, rows), BF16),
            pltpu.VMEM((line, 2, width, rows), BF16),
            pltpu.VMEM((chunks, line, width, chunk), F32),
            pltpu.VMEM((width, wide), BF16),
            pltpu.VMEM((width, wide), BF16),
            pltpu.VMEM((rows, inner - wide), BF16),
            pltpu.VMEM((rows, inner - wide), BF16),
            pltpu.VMEM((rows, inner), BF16),
            pltpu.VMEM((rows, inner), BF16),
            pltpu.VMEM((line, 2, width, inner), BF16),
            pltpu.VMEM((line, 2, width, rows), F32),
            pltpu.VMEM((line, 2, width, rows), F32),
            pltpu.VMEM((line, width, rows), F32),
            pltpu.VMEM((columns, rows), F32),
            pltpu.VMEM((groups, GROUP, rows), F32),
            pltpu.VMEM((groups, GROUP, rows), F32),
            pltpu.VMEM((groups, GROUP, rows), F32),
            pltpu.VMEM((groups, GROUP, rows), F32),
            pltpu.VMEM((rows, rows), F32),
            pltpu.VMEM((rows, rows), F32),
            pltpu.VMEM((heads, rows), BF16),
            pltpu.VMEM((heads, rows), BF16),
            pltpu.VMEM((rows, inner), F32),
            pltpu.VMEM((2, line, width, rows), BF16),
            pltpu.VMEM((line, width, rows), BF16),
            pltpu.VMEM((chunks, line, width, chunk), BF16),
            pltpu.VMEM((chunks, line, width, chunk), BF16),
            pltpu.VMEM((chunks, line, width, chunk), BF16),
            pltpu.VMEM((chunks, line, width, chunk), BF16),
            dma, dma, dma, dma((line,)), dma((line,)), dma((line,)), dma((line,)), dma((line,)), dma((2,)), dma((2,)),
            dma((2,)), dma((2,)), dma((line,)), dma((line,)), dma((line,)),
            dma((line,)), dma((line,)), dma((line,)), dma((line,)), dma((2,)), dma((2,)),
            dma((2,)), dma((2,)), dma((chunks, line)), dma((chunks, line)), dma((chunks, line)),
            dma((chunks, line)),
        ],
        compiler_params=pltpu.CompilerParams(
            collective_id=0, has_side_effects=True, vmem_limit_bytes=60 * 1024 * 1024
        ),
    )(
        inputs,
        returned[0],
        proj_weight[0].T,
        log_rate,
        step_bias,
        skip_gain,
    )
    return (grad_out[None], share.T[None])


def solution(mesh):
    placed = (
        P("pp", "fsdp", "tp"),
        P("pp", "fsdp", "tp"),
        P("pp", "tp", "fsdp"),
        P("pp", "tp"),
        P("pp", "tp"),
        P("pp", "tp"),
    )
    return jax.shard_map(
        fused_device if fits(mesh) else per_device,
        mesh=mesh,
        in_specs=placed,
        out_specs=(P("pp", "fsdp", "tp"), P("pp", "tp", "fsdp")),
        check_vma=False,
    )
```

```python
import functools

import jax
import jax.numpy as jnp
from jax import lax
from jax.experimental import pallas as pl
from jax.experimental.pallas import tpu as pltpu
from jax.sharding import PartitionSpec as P

HEAD_DIM = 64
STATE = 256
BLOCK = 128


def shifted(value, axis, by):
    count = lax.axis_size(axis)
    return lax.ppermute(value, axis, [(i, (i + by) % count) for i in range(count)])


def state_space(head_input, b_values, c_values, raw_step, log_rate, step_bias, skip_gain):
    length, head_count, head_size = head_input.shape
    blocks = length // BLOCK
    highest = lax.Precision.HIGHEST
    step_size = jax.nn.softplus(raw_step + step_bias[None, :])
    log_decay = -step_size * jnp.exp(log_rate)[None, :]
    block_values = head_input.reshape(blocks, BLOCK, head_count, head_size)
    b_blocks = b_values.reshape(blocks, BLOCK, b_values.shape[1])
    c_blocks = c_values.reshape(blocks, BLOCK, c_values.shape[1])
    cumulative = jnp.cumsum(log_decay.reshape(blocks, BLOCK, head_count), axis=1)
    scaled = block_values * step_size.reshape(blocks, BLOCK, head_count)[..., None]
    scores = jnp.einsum("kin,kjn->kij", c_blocks, b_blocks, precision=highest)
    causal = (jnp.arange(BLOCK)[:, None] >= jnp.arange(BLOCK)[None, :])[None, :, :, None]
    log_gaps = cumulative[:, :, None, :] - cumulative[:, None, :, :]
    mixing = jnp.where(causal, jnp.exp(jnp.where(causal, log_gaps, 0.0)), 0.0) * scores[..., None]
    within = jnp.einsum("kijh,kjhp->kihp", mixing, scaled, precision=highest)
    to_end = jnp.exp(cumulative[:, -1:, :] - cumulative)
    states = jnp.einsum("kjn,kjhp->khnp", b_blocks, scaled * to_end[..., None], precision=highest)
    totals = jnp.exp(cumulative[:, -1, :])

    def advance(running, inputs_pair):
        block_state, block_total = inputs_pair
        return (block_total[:, None, None] * running + block_state, running)

    start_state = jnp.zeros((head_count, b_values.shape[1], head_size), head_input.dtype)
    _, entering = lax.scan(advance, start_state, (states, totals))
    across = (
        jnp.einsum("kin,khnp->kihp", c_blocks, entering, precision=highest)
        * jnp.exp(cumulative)[..., None]
    )
    output = (within + across).reshape(length, head_count, head_size)
    return output + skip_gain[None, :, None] * head_input


def head_share(partial_sums):
    return lax.psum_scatter(partial_sums, "tp", scatter_dimension=0, tiled=True)


def per_device(saved_inputs, returned, proj_weight, log_rate, step_bias, skip_gain):
    inputs = saved_inputs[0]
    row_count, inner_here = inputs.shape
    heads_here = log_rate.shape[1]
    weight_local = proj_weight[0]
    arrived = shifted(returned, "pp", -1)[0]
    weight_full = lax.all_gather(weight_local, "fsdp", axis=1, tiled=True)
    partial_proj = jnp.dot(inputs, weight_full, preferred_element_type=jnp.float32)
    projected = lax.all_gather(head_share(partial_proj), "tp", axis=0, tiled=True)
    head_total = projected.shape[1] - 2 * STATE
    offset = lax.axis_index("tp") * heads_here
    raw_step = lax.dynamic_slice_in_dim(projected, 2 * STATE + offset, heads_here, 1)
    values = inputs.astype(jnp.float32).reshape(row_count, heads_here, HEAD_DIM)

    def local_core(head_input, b_values, c_values, step_raw):
        return state_space(
            head_input, b_values, c_values, step_raw, log_rate[0], step_bias[0], skip_gain[0]
        )

    _, backward = jax.vjp(
        local_core, values, projected[:, :STATE], projected[:, STATE : 2 * STATE], raw_step
    )
    upstream = arrived.astype(jnp.float32)
    grad_x, grad_b, grad_c, grad_raw = backward(upstream.reshape(row_count, heads_here, HEAD_DIM))
    placed = lax.dynamic_update_slice_in_dim(
        jnp.zeros((row_count, head_total), jnp.float32), grad_raw, offset, 1
    )
    grad_share = head_share(jnp.concatenate([grad_b, grad_c, placed], axis=1)).astype(jnp.bfloat16)
    proj_grad = lax.all_gather(grad_share, "tp", axis=0, tiled=True)
    back_proj = lax.dot_general(
        proj_grad, weight_full, (((1,), (1,)), ((), ())), preferred_element_type=jnp.float32
    )
    grad_inputs = (upstream + grad_x.reshape(row_count, inner_here) + back_proj).astype(
        jnp.bfloat16
    )
    share = lax.psum_scatter(
        lax.dot_general(
            proj_grad, inputs, (((0,), (0,)), ((), ())), preferred_element_type=jnp.float32
        ),
        "fsdp",
        scatter_dimension=0,
        tiled=True,
    )
    section_wgrad = share.T
    return (grad_inputs[None], section_wgrad[None])


MESH = pl.DeviceIdType.MESH
F32 = jnp.float32
BF16 = jnp.bfloat16
GROUP = 8


def fits(mesh):
    return mesh.shape["tp"] == 2 and mesh.shape["fsdp"] == 8


def times(left, right, over, precision=None):
    return lax.dot_general(
        left, right, ((over[:1], over[1:]), ((), ())),
        precision=precision, preferred_element_type=F32,
    )


def fused_kernel(
    line, pairs,
    x_hbm, ret_ref, w_ref, rate_ref, bias_ref, gain_ref,
    out_ref, wg_ref,
    x_ref, gain_s, xa, pg_z, pg_a, parts, side_out, side_in, bp_out, bp_in,
    arrived, x_other, w_all, proj, proj_tp, proj_theirs, projs,
    shift_s, cum_s, dshift_s, rs_s, ds_s, ds_in, raw_out, raw_in, gx,
    pg_x, pg_in, up_out, dn_out, up_in, dn_in,
    local_sem, local_x, local_a, xa_recv, xa_up, xa_dn, pa_send, pa_recv, side_sem, bp_sem, ret_sem, x_sem, wz_recv, wz_up, wz_dn, wx_send, wx_recv,
    pj_send, pj_recv, tp_sem, ds_sem, raw_sem, pg_sem, up_send, up_recv, dn_send, dn_recv,
):
    exact = lax.Precision.HIGHEST
    pp_count = lax.axis_size("pp")
    pp, f, tp = lax.axis_index("pp"), lax.axis_index("fsdp"), lax.axis_index("tp")
    z, x = f // 2, f % 2
    width, inner = w_ref.shape
    rows = x_ref.shape[0]
    heads = rate_ref.shape[1]
    wide = xa.shape[2]
    last = line - 1
    before = {"pp": lax.rem(pp + pp_count - 1, pp_count)}
    after = {"pp": lax.rem(pp + 1, pp_count)}
    side = {"fsdp": f + 1 - 2 * x}
    core = {"tp": 1 - tp}
    above, below = {"fsdp": f + 2}, {"fsdp": f - 2}

    def remote(src, dst, send, recv, where):
        return pltpu.make_async_remote_copy(
            src_ref=src, dst_ref=dst, send_sem=send, recv_sem=recv,
            device_id=where, device_id_type=MESH,
        )

    barrier = pltpu.get_barrier_semaphore()
    greeted = [side, core, before] + ([after] if pairs > 2 else [])
    for where in greeted:
        pl.semaphore_signal(barrier, inc=1, device_id=where, device_id_type=MESH)

    for k in range(1, line):
        along = {"fsdp": 2 * lax.rem(z + k, line) + x}
        pl.semaphore_signal(barrier, inc=1, device_id=along, device_id_type=MESH)
    pl.semaphore_wait(barrier, len(greeted) + line - 1)

    own_w = pltpu.make_async_copy(w_ref, w_all.at[z, x], local_sem)
    own_x = pltpu.make_async_copy(x_hbm, x_ref, local_x)
    own_a = pltpu.make_async_copy(x_hbm.at[:, pl.ds(0, wide)], xa.at[z], local_a)

    def w_up(block, s):
        src = w_ref if s == 0 else w_all.at[block, x]
        return remote(src, w_all.at[block, x], wz_up.at[s], wz_recv.at[block], above)

    def w_dn(block, s):
        src = w_ref if s == 0 else w_all.at[block, x]
        return remote(src, w_all.at[block, x], wz_dn.at[s], wz_recv.at[block], below)

    def w_side(block, column=x):
        half = w_all.at[block, column, :, pl.ds(0, wide)]
        return remote(half, half, wx_send.at[block], wx_recv.at[block], side)

    @pl.when(z < last)
    def _():
        w_up(z, 0).start()

    @pl.when(z > 0)
    def _():
        w_dn(z, 0).start()

    x_copy = remote(x_hbm, x_other, x_sem.at[0], x_sem.at[1], side)
    x_copy.start()
    ret_copy = remote(ret_ref, arrived, ret_sem.at[0], ret_sem.at[1], before)
    ret_copy.start()
    own_w.start()
    own_x.start()
    own_a.start()

    def pj_copy(block):
        return remote(
            proj_theirs.at[block], proj.at[block, x], pj_send.at[block], pj_recv.at[block], side
        )

    def project(block):
        weight = w_all[block, x]
        proj_theirs[block] = times(weight, x_other[...], (1, 1))
        pj_copy(block).start()
        proj[block, x] = times(weight, x_ref[...], (1, 1))

    def xa_up_copy(block, s):
        return remote(xa.at[block], xa.at[block], xa_up.at[s], xa_recv.at[block], above)

    def xa_dn_copy(block, s):
        return remote(xa.at[block], xa.at[block], xa_dn.at[s], xa_recv.at[block], below)

    def xa_pass(s):
        low, high = z - s, z + s

        @pl.when(low >= 0)
        def _():
            xa_dn_copy(low, s - 1).wait_recv()
            if s < line - 1:
                @pl.when(z < last)
                def _():
                    xa_up_copy(low, s).start()

        @pl.when(high <= last)
        def _():
            xa_up_copy(high, s - 1).wait_recv()
            if s < line - 1:
                @pl.when(z > 0)
                def _():
                    xa_dn_copy(high, s).start()

    def w_pass(s):
        low, high = z - s, z + s

        @pl.when(low >= 0)
        def _():
            w_dn(low, s - 1).wait_recv()
            if s < line - 1:
                @pl.when(z < last)
                def _():
                    w_up(low, s).start()

        @pl.when(high <= last)
        def _():
            w_up(high, s - 1).wait_recv()
            if s < line - 1:
                @pl.when(z > 0)
                def _():
                    w_dn(high, s).start()

        @pl.when(jnp.logical_and(z == s - 1, z < last))
        def _():
            xa_up_copy(z, 0).start()

        @pl.when(jnp.logical_and(z == last + 1 - s, z > 0))
        def _():
            xa_dn_copy(z, 0).start()

    def project_at(s):
        @pl.when(z - s >= 0)
        def _():
            project(z - s)

        @pl.when(z + s <= last)
        def _():
            project(z + s)

    own_w.wait()
    own_x.wait()
    own_a.wait()
    w_pass(1)
    x_copy.wait_recv()
    w_side(z).start()
    project(z)
    for low_or_high in (z - 1, z + 1):
        @pl.when(jnp.logical_and(low_or_high >= 0, low_or_high <= last))
        def _():
            w_side(low_or_high).start()

    w_pass(2)
    project_at(1)
    for s in range(3, line):
        w_pass(s)
        project_at(s - 1)
    project_at(line - 1)
    for block in range(line):
        remote(
            proj_theirs.at[block], proj.at[block, 1 - x], pj_send.at[block], pj_recv.at[block], side
        ).wait_recv()
    tp_copy = remote(proj, proj_tp, tp_sem.at[0], tp_sem.at[1], core)
    tp_copy.start()
    tp_copy.wait_recv()
    projs[...] = (proj[...] + proj_tp[...]).reshape(projs.shape)

    for block in range(line):
        @pl.when(jnp.logical_or(block > z + 1, block < z - 1))
        def _():
            w_side(block).start()

    row_at = lax.broadcasted_iota(jnp.int32, (rows, rows), 0)
    column_at = lax.broadcasted_iota(jnp.int32, (rows, rows), 1)
    lower = (row_at >= column_at).astype(F32)
    causal = row_at <= column_at
    upper = (row_at <= column_at).astype(F32)
    b_t, c_t = projs[:STATE], projs[STATE : 2 * STATE]
    start = pl.multiple_of(2 * STATE + tp * heads, 8)
    raw = projs[pl.ds(start, heads)] + jnp.broadcast_to(bias_ref[...], (rows, heads)).T
    step = jnp.maximum(raw, 0.0) + jnp.log1p(jnp.exp(-jnp.abs(raw)))
    decay = -jnp.exp(jnp.broadcast_to(rate_ref[...], (rows, heads)).T)
    groups = heads // GROUP
    gain_s[...] = jnp.broadcast_to(gain_ref[...], (rows, heads)).T.reshape(groups, GROUP, rows)
    cumulative = times(step * decay, upper, (1, 0), exact)
    cum_s[...] = cumulative.reshape(groups, GROUP, rows)
    shift_s[...] = (cumulative - jnp.log(step)).reshape(groups, GROUP, rows)
    head_of = lax.broadcasted_iota(jnp.int32, (GROUP, GROUP * HEAD_DIM), 1) // HEAD_DIM
    picks = (head_of == lax.broadcasted_iota(jnp.int32, head_of.shape, 0)).astype(F32).astype(BF16)
    scores = times(b_t, c_t, (0, 0), exact)
    scores = jnp.concatenate([scores, scores], axis=1)
    ds_s[...] = jnp.zeros_like(ds_s)
    pair_lanes = 2 * HEAD_DIM
    lane = lax.broadcasted_iota(jnp.int32, (rows, pair_lanes), 1)
    ret_copy.wait_recv()

    def group_step(g, carry):
        cum_rows = cum_s[g]
        shift_columns = shift_s[g].T
        gain_rows = gain_s[g]

        @pl.when(g == groups // 4)
        def _():
            xa_pass(1)

        rs_rows, shares, ds_part = [], [], None
        for p in range(GROUP // 2):
            at = pl.multiple_of(g * (GROUP * HEAD_DIM) + p * pair_lanes, pair_lanes)
            g_wide = arrived[:, pl.ds(at, pair_lanes)].astype(F32)
            x_pair = x_ref[:, pl.ds(at, pair_lanes)]
            g_both = jnp.concatenate(
                [
                    jnp.where(lane < HEAD_DIM, g_wide, 0.0).astype(BF16),
                    jnp.where(lane < HEAD_DIM, 0.0, g_wide).astype(BF16),
                ],
                axis=0,
            )
            products = times(x_pair, g_both, (1, 1))
            masks = []
            for h in (2 * p, 2 * p + 1):
                gap = cum_rows[h : h + 1] - shift_columns[:, h : h + 1]
                masks.append(jnp.exp(jnp.where(causal, gap, -1e30)))
            mask = jnp.concatenate(masks, axis=1)
            mixed = mask * scores
            sums = jnp.sum(mixed * products, axis=0, keepdims=True)
            rs_rows += [sums[:, :rows], sums[:, rows:]]
            weighted = mask * products
            weighted = weighted[:, :rows] + weighted[:, rows:]
            ds_part = weighted if ds_part is None else ds_part + weighted
            dx = times(mixed.astype(BF16), g_both, (1, 0))
            gain = jnp.where(
                lane[:1] < HEAD_DIM, gain_rows[2 * p : 2 * p + 1], gain_rows[2 * p + 1 : 2 * p + 2]
            )
            gx[:, pl.ds(at, pair_lanes)] = dx + (1.0 + gain) * g_wide
            shares.append(dx * x_pair.astype(F32))
        ds_s[...] += ds_part
        share = jnp.concatenate(shares, axis=1)
        high = share.astype(BF16)
        low = (share - high.astype(F32)).astype(BF16)
        dshift_s[g] = times(picks, high, (1, 1)) + times(picks, low, (1, 1))
        rs_s[g] = jnp.concatenate(rs_rows, axis=0)
        return carry

    lax.fori_loop(0, groups, group_step, 0)
    ds_copy = remote(ds_s, ds_in, ds_sem.at[0], ds_sem.at[1], core)
    ds_copy.start()
    xa_pass(2)
    ddt = dshift_s[...].reshape(heads, rows)
    d_cum = rs_s[...].reshape(heads, rows) - ddt
    d_decay = times(d_cum, lower, (1, 0), exact)
    slope = jnp.exp(jnp.minimum(raw, 0.0)) / (1.0 + jnp.exp(-jnp.abs(raw)))
    ratio = jnp.where(step > 1e-30, slope / jnp.maximum(step, 1e-30), 1.0)
    raw_out[...] = (ddt * ratio + d_decay * decay * slope).astype(BF16)
    raw_copy = remote(raw_out, raw_in, raw_sem.at[0], raw_sem.at[1], core)
    raw_copy.start()
    ds_copy.wait_recv()
    ds_total = ds_s[...] + ds_in[...]
    grad_b = times(c_t, ds_total, (1, 1), exact).astype(BF16)
    grad_c = times(b_t, ds_total, (1, 0), exact).astype(BF16)
    raw_copy.wait_recv()
    mine, other = raw_out[...].astype(F32), raw_in[...].astype(F32)
    first = jnp.where(tp == 0, mine, other).astype(BF16)
    second = jnp.where(tp == 0, other, mine).astype(BF16)
    proj_grad = jnp.concatenate([grad_b, grad_c, first, second], axis=0)
    pg_z[...] = proj_grad.reshape(line, 2, width, rows)
    pg_x[...] = jnp.stack([pg_z[:, 0], pg_z[:, 1]], axis=0)
    pg_copy = remote(pg_x.at[1 - x], pg_in, pg_sem.at[0], pg_sem.at[1], side)
    pg_copy.start()

    def pa_copy(k):
        to = lax.rem(z + k, line)
        return remote(
            pg_z.at[to], pg_a.at[z], pa_send.at[k], pa_recv.at[k], {"fsdp": 2 * to + x}
        )

    for k in range(1, line):
        pa_copy(k).start()
    turned = proj_grad.astype(F32).T.astype(BF16)
    pg_a[z] = pg_z[z]
    pg_copy.wait_recv()

    tile = 512
    chunk = parts.shape[3]
    chunks = parts.shape[0]
    both = jnp.concatenate(
        [pg_x[x].reshape(line * width, rows), pg_in[...].reshape(line * width, rows)], axis=1
    )

    def part(c):
        def body(i, carry):
            at = pl.multiple_of(i * tile, tile)
            here = pl.multiple_of(wide + c * chunk + i * tile, tile)
            tokens = jnp.concatenate(
                [x_ref[:, pl.ds(here, tile)], x_other[:, pl.ds(here, tile)]], axis=0
            )
            value = times(both, tokens, (1, 0))
            parts[c, :, :, pl.ds(at, tile)] = value.reshape(line, width, tile)
            return carry

        lax.fori_loop(0, chunk // tile, body, 0)

    def turn(value):
        return value.reshape(line * width, rows).astype(F32).T.astype(BF16)

    bp_copy = remote(bp_out, bp_in, bp_sem.at[0], bp_sem.at[1], side)
    turned_in = turn(pg_in[...])
    turned_own = turn(pg_x[x])

    def back_other(i, carry):
        at = pl.multiple_of(i * tile, tile)
        far = pl.multiple_of(wide + i * tile, tile)
        weight = w_all[:, x, :, pl.ds(far, tile)].reshape(line * width, tile)
        bp_out[:, pl.ds(at, tile)] = times(turned_in, weight, (1, 0)).astype(BF16)
        return carry

    def up_copy(c, block, where=above):
        return remote(
            up_out.at[c, block], up_in.at[c, block], up_send.at[c, block], up_recv.at[c, block],
            where,
        )

    def dn_copy(c, block, where=below):
        return remote(
            dn_out.at[c, block], dn_in.at[c, block], dn_send.at[c, block], dn_recv.at[c, block],
            where,
        )

    for c in range(chunks):
        part(c)

        @pl.when(z == 0)
        def _():
            for block in range(last, 0, -1):
                up_out[c, block] = parts[c, block].astype(BF16)
                up_copy(c, block).start()

        @pl.when(z == last)
        def _():
            for block in range(last):
                dn_out[c, block] = parts[c, block].astype(BF16)
                dn_copy(c, block).start()

    lax.fori_loop(0, (inner - wide) // tile, back_other, 0)
    bp_copy.start()
    for k in range(1, line):
        src = lax.rem(z + line - k, line)
        remote(
            pg_z.at[z], pg_a.at[src], pa_send.at[k], pa_recv.at[k], {"fsdp": 2 * src + x}
        ).wait_recv()
    xa_pass(3)
    mine_a = jnp.concatenate([pg_a[b, x] for b in range(line)], axis=1)
    side_a = jnp.concatenate([pg_a[b, 1 - x] for b in range(line)], axis=1)
    all_a = jnp.concatenate([mine_a, side_a], axis=0)

    def gathered(i, carry):
        at = pl.multiple_of(i * tile, tile)
        tokens = xa[:, :, pl.ds(at, tile)].reshape(line * rows, tile)
        value = times(all_a, tokens, (1, 0))
        wg_ref[:, pl.ds(at, tile)] = value[:width]
        side_out[:, pl.ds(at, tile)] = value[width:].astype(BF16)
        return carry

    lax.fori_loop(0, wide // tile, gathered, 0)
    side_copy = remote(side_out, side_in, side_sem.at[0], side_sem.at[1], side)
    side_copy.start()

    def relay(c):
        for k in range(last):
            up_block, dn_block = last - k, k

            @pl.when(jnp.logical_and(z > 0, z < up_block))
            def _():
                up_copy(c, up_block, below).wait_recv()
                up_out[c, up_block] = (
                    parts[c, up_block] + up_in[c, up_block].astype(F32)
                ).astype(BF16)
                up_copy(c, up_block).start()

            @pl.when(jnp.logical_and(z < last, z > dn_block))
            def _():
                dn_copy(c, dn_block, above).wait_recv()
                dn_out[c, dn_block] = (
                    parts[c, dn_block] + dn_in[c, dn_block].astype(F32)
                ).astype(BF16)
                dn_copy(c, dn_block).start()

    def back(i, carry):
        at = pl.multiple_of(i * tile, tile)
        weight = w_all[:, :, :, pl.ds(at, tile)].reshape(line * 2 * width, tile)
        out_ref[:, pl.ds(at, tile)] = (
            gx[:, pl.ds(at, tile)] + times(turned, weight, (1, 0))
        ).astype(BF16)
        return carry

    for c in range(chunks // 2):
        relay(c)
    for block in range(line):
        w_side(block, 1 - x).wait_recv()
    lax.fori_loop(0, wide // tile, back, 0)
    for c in range(chunks // 2, chunks - 1):
        relay(c)
    bp_copy.wait_recv()

    def back_far(i, carry):
        at = pl.multiple_of(i * tile, tile)
        far = pl.multiple_of(wide + i * tile, tile)
        weight = w_all[:, x, :, pl.ds(far, tile)].reshape(line * width, tile)
        out_ref[:, pl.ds(far, tile)] = (
            gx[:, pl.ds(far, tile)]
            + times(turned_own, weight, (1, 0))
            + bp_in[:, pl.ds(at, tile)].astype(F32)
        ).astype(BF16)
        return carry

    lax.fori_loop(0, (inner - wide) // tile, back_far, 0)
    relay(chunks - 1)
    side_copy.wait_recv()
    wg_ref[:, :wide] = wg_ref[:, :wide] + side_in[...].astype(F32)
    for c in range(chunks):
        lanes = slice(wide + c * chunk, wide + (c + 1) * chunk)

        @pl.when(z > 0)
        def _():
            up_copy(c, z, below).wait_recv()

        @pl.when(z < last)
        def _():
            dn_copy(c, z, above).wait_recv()

        @pl.when(z == 0)
        def _():
            wg_ref[:, lanes] = parts[c, z] + dn_in[c, z].astype(F32)

        @pl.when(z == last)
        def _():
            wg_ref[:, lanes] = parts[c, z] + up_in[c, z].astype(F32)

        @pl.when(jnp.logical_and(z > 0, z < last))
        def _():
            wg_ref[:, lanes] = (
                parts[c, z] + up_in[c, z].astype(F32) + dn_in[c, z].astype(F32)
            )

    for copy in (x_copy, ret_copy, tp_copy, ds_copy, raw_copy, pg_copy, side_copy, bp_copy):
        copy.wait_send()
    for block in range(line):
        pj_copy(block).wait_send()
        w_side(block).wait_send()

        for c in range(chunks):
            @pl.when(block > z)
            def _():
                up_copy(c, block).wait_send()

            @pl.when(block < z)
            def _():
                dn_copy(c, block).wait_send()

    for k in range(1, line):
        pa_copy(k).wait_send()

    for s in range(line - 1):
        @pl.when(jnp.logical_and(z < last, z - s >= 0))
        def _():
            w_up(z - s, s).wait_send()
            xa_up_copy(z - s, s).wait_send()

        @pl.when(jnp.logical_and(z > 0, z + s <= last))
        def _():
            w_dn(z + s, s).wait_send()
            xa_dn_copy(z + s, s).wait_send()


def fused_device(saved_inputs, returned, proj_weight, log_rate, step_bias, skip_gain):
    inputs = saved_inputs[0]
    rows, inner = inputs.shape
    heads = log_rate.shape[1]
    width = proj_weight.shape[2]
    line = lax.axis_size("fsdp") // 2
    columns = line * 2 * width
    groups = heads // GROUP
    wide = inner // 2
    chunks = 4
    chunk = (inner - wide) // chunks
    vmem = pl.BlockSpec(memory_space=pltpu.VMEM)
    dma = pltpu.SemaphoreType.DMA
    grad_out, share = pl.pallas_call(
        functools.partial(fused_kernel, line, lax.axis_size("pp")),
        out_shape=(
            jax.ShapeDtypeStruct((rows, inner), BF16),
            jax.ShapeDtypeStruct((width, inner), F32),
        ),
        in_specs=[pl.BlockSpec(memory_space=pl.ANY)] * 3 + [vmem] * 3,
        out_specs=(vmem, vmem),
        scratch_shapes=[
            pltpu.VMEM((rows, inner), BF16),
            pltpu.VMEM((groups, GROUP, rows), F32),
            pltpu.VMEM((line, rows, wide), BF16),
            pltpu.VMEM((line, 2, width, rows), BF16),
            pltpu.VMEM((line, 2, width, rows), BF16),
            pltpu.VMEM((chunks, line, width, chunk), F32),
            pltpu.VMEM((width, wide), BF16),
            pltpu.VMEM((width, wide), BF16),
            pltpu.VMEM((rows, inner - wide), BF16),
            pltpu.VMEM((rows, inner - wide), BF16),
            pltpu.VMEM((rows, inner), BF16),
            pltpu.VMEM((rows, inner), BF16),
            pltpu.VMEM((line, 2, width, inner), BF16),
            pltpu.VMEM((line, 2, width, rows), F32),
            pltpu.VMEM((line, 2, width, rows), F32),
            pltpu.VMEM((line, width, rows), F32),
            pltpu.VMEM((columns, rows), F32),
            pltpu.VMEM((groups, GROUP, rows), F32),
            pltpu.VMEM((groups, GROUP, rows), F32),
            pltpu.VMEM((groups, GROUP, rows), F32),
            pltpu.VMEM((groups, GROUP, rows), F32),
            pltpu.VMEM((rows, rows), F32),
            pltpu.VMEM((rows, rows), F32),
            pltpu.VMEM((heads, rows), BF16),
            pltpu.VMEM((heads, rows), BF16),
            pltpu.VMEM((rows, inner), F32),
            pltpu.VMEM((2, line, width, rows), BF16),
            pltpu.VMEM((line, width, rows), BF16),
            pltpu.VMEM((chunks, line, width, chunk), BF16),
            pltpu.VMEM((chunks, line, width, chunk), BF16),
            pltpu.VMEM((chunks, line, width, chunk), BF16),
            pltpu.VMEM((chunks, line, width, chunk), BF16),
            dma, dma, dma, dma((line,)), dma((line,)), dma((line,)), dma((line,)), dma((line,)), dma((2,)), dma((2,)),
            dma((2,)), dma((2,)), dma((line,)), dma((line,)), dma((line,)),
            dma((line,)), dma((line,)), dma((line,)), dma((line,)), dma((2,)), dma((2,)),
            dma((2,)), dma((2,)), dma((chunks, line)), dma((chunks, line)), dma((chunks, line)),
            dma((chunks, line)),
        ],
        compiler_params=pltpu.CompilerParams(
            collective_id=0, has_side_effects=True, vmem_limit_bytes=60 * 1024 * 1024
        ),
    )(
        inputs,
        returned[0],
        proj_weight[0].T,
        log_rate,
        step_bias,
        skip_gain,
    )
    return (grad_out[None], share.T[None])


def solution(mesh):
    placed = (
        P("pp", "fsdp", "tp"),
        P("pp", "fsdp", "tp"),
        P("pp", "tp", "fsdp"),
        P("pp", "tp"),
        P("pp", "tp"),
        P("pp", "tp"),
    )
    return jax.shard_map(
        fused_device if fits(mesh) else per_device,
        mesh=mesh,
        in_specs=placed,
        out_specs=(P("pp", "fsdp", "tp"), P("pp", "tp", "fsdp")),
        check_vma=False,
    )
```
